128 devices in a mesh: dp: 8 (over x, z_lo), tensor: 16 (over z_hi, y, core).
Axes of the slice: x: 4, y: 4, z: 4 (z_hi: 2, z_lo: 2; z = z_hi * 2 + z_lo), core: 2. Of those that a mesh axis runs over, the one named last changes fastest.
Arguments:
- text_grads: bfloat16 [8, 8192, 2048], P('dp', 'tensor'), may hold values from -6 to 6
- text_master: float32 [8192, 2048], P('tensor', 'dp'), may hold values from -2 to 2
- text_moment: float32 [8192, 2048], P('tensor', 'dp'), may hold values from -4 to 4
- text_second: float32 [8192, 2048], P('tensor', 'dp'), may hold values from 0.01 to 1
- text_ref: float32 [8192, 2048], P('tensor', 'dp'), may hold values from -2 to 2
- vision_grads: bfloat16 [128, 2, 1280, 1280], P(('dp', 'tensor')), may hold values from -6 to 6
- vision_master: float32 [2, 1280, 1280], P(None, ('dp', 'tensor')), may hold values from -2 to 2
- vision_moment: float32 [2, 1280, 1280], P(None, ('dp', 'tensor')), may hold values from -4 to 4
- vision_second: float32 [2, 1280, 1280], P(None, ('dp', 'tensor')), may hold values from 0.01 to 1
- vision_ref: float32 [2, 1280, 1280], P(None, ('dp', 'tensor')), may hold values from -2 to 2
Outputs:
- text_master_new: float32 [8192, 2048], P('tensor', 'dp')
- text_moment_new: float32 [8192, 2048], P('tensor', 'dp')
- text_second_new: float32 [8192, 2048], P('tensor', 'dp')
- text_ref_new: float32 [8192, 2048], P('tensor', 'dp')
- text_weights: bfloat16 [8192, 2048], P('tensor')
- vision_master_new: float32 [2, 1280, 1280], P(None, ('dp', 'tensor'))
- vision_moment_new: float32 [2, 1280, 1280], P(None, ('dp', 'tensor'))
- vision_second_new: float32 [2, 1280, 1280], P(None, ('dp', 'tensor'))
- vision_ref_new: float32 [2, 1280, 1280], P(None, ('dp', 'tensor'))
- vision_weights: bfloat16 [2, 1280, 1280], replicated
The draws below stay inside these ranges and needn't reach their ends.
All inputs are finite; a program needn't handle non-finite values.
Results may differ from the reference program's by a relative error of at most 0.012.
Values may be sent and summed in bfloat16 or wider, within the bound.
A program may use at most 128 MiB of HBM per device.

```python
import math
import jax
import jax.numpy as jnp
from jax import lax

D = 8192
VW = 1280
VL = 2
KVW = 2048
N_DP = 8
DEVICES = 128


def spiked(drawn, key, source, target, parts, factor):
    def block_of(position):
        return (jnp.arange(drawn.shape[position]) // (drawn.shape[position] // parts)).reshape((-1,) + (1,) * (drawn.ndim - 1 - position))

    one_side = jax.random.permutation(key, parts)[block_of(target)]
    second = (block_of(target) + parts // 2) % parts
    return jnp.where((block_of(source) == one_side) | (block_of(source) == second), factor * drawn, drawn)


def shard_levels(key, extent, shards, least, high):
    level = 1.0
    for dim, shards_of in shards:
        heights = jax.random.uniform(jax.random.fold_in(jax.random.fold_in(key, 6), dim), (shards_of,), jnp.float32, least / len(shards), high / len(shards))
        level = level * jnp.repeat(jnp.exp(heights), extent[dim] // shards_of).reshape((-1,) + (1,) * (len(extent) - 1 - dim))
    return level


def gaussian(stream_key, extent, width, bound, shards=(), dtype=jnp.bfloat16):
    values = width * jax.random.normal(stream_key, extent, jnp.float32)
    if shards:
        values = values * shard_levels(stream_key, extent, shards, -0.22, 0.18)
    return jnp.clip(values, -bound, bound).astype(dtype)


def bell_draw_with(stream_key, extent, spread, most, shards, heavy, held_as=jnp.bfloat16):
    entries = spread * jax.random.normal(stream_key, extent, jnp.float32)
    if shards:
        entries = entries * shard_levels(stream_key, extent, shards, -0.22, 0.18)
    return jnp.clip(spiked(entries, jax.random.fold_in(stream_key, 3), *heavy), -most, most).astype(held_as)


def setup_inputs(seed: int = 0) -> dict:
    key_of = jax.random.split(jax.random.key(seed), 11)
    text_grads = bell_draw_with(key_of[0], (N_DP, D, KVW), 0.3, 6.0, ((0, 8), (1, 16)), (0, 2, 8, 2.0))
    text_master = gaussian(key_of[1], (D, KVW), 0.15, 2.0, ((0, 16), (1, 8)), jnp.float32)
    text_moment = gaussian(key_of[2], (D, KVW), 0.3, 4.0, ((0, 16), (1, 8)), jnp.float32)
    text_second = jnp.clip(jnp.exp(math.log(1.0) - 4.6051702 * jax.random.uniform(key_of[3], (D, KVW), jnp.float32) ** shard_levels(key_of[3], (D, KVW), ((0, 16), (1, 8)), -0.2, 0.2)), 0.01, 1.0)
    text_ref = gaussian(key_of[4], (D, KVW), 0.15, 2.0, ((0, 16), (1, 8)), jnp.float32)
    vision_grads = bell_draw_with(key_of[5], (DEVICES, VL, VW, VW), 0.3, 6.0, ((0, 128),), (0, 2, 128, 5.5))
    vision_master = gaussian(key_of[6], (VL, VW, VW), 0.15, 2.0, ((1, 128),), jnp.float32)
    vision_moment = gaussian(key_of[7], (VL, VW, VW), 0.3, 4.0, ((1, 128),), jnp.float32)
    vision_second = jnp.clip(jnp.exp(math.log(1.0) - 4.6051702 * jax.random.uniform(key_of[8], (VL, VW, VW), jnp.float32) ** shard_levels(key_of[8], (VL, VW, VW), ((1, 128),), -0.2, 0.2)), 0.01, 1.0)
    vision_ref = gaussian(key_of[9], (VL, VW, VW), 0.15, 2.0, ((1, 128),), jnp.float32)
    return {"text_grads": text_grads, "text_master": text_master, "text_moment": text_moment, "text_second": text_second, "text_ref": text_ref, "vision_grads": vision_grads, "vision_master": vision_master, "vision_moment": vision_moment, "vision_second": vision_second, "vision_ref": vision_ref}


beta_one = 0.9
beta_two = 0.95
correct_one = 1.0 - 0.9 ** 10
correct_two = 1.0 - 0.95 ** 10
learn_rate = 0.01
decay_rate = 0.1
blend_rate = 0.6

def adam_step(grad, moment, second, master, refcopy):
    moment_new = beta_one * moment + (1.0 - beta_one) * grad
    second_new = beta_two * second + (1.0 - beta_two) * grad * grad
    update = moment_new / correct_one / (jnp.sqrt(second_new / correct_two) + 1e-08)
    master_new = master - learn_rate * (update + decay_rate * master)
    ref_new = blend_rate * master_new + (1.0 - blend_rate) * refcopy
    return (master_new, moment_new, second_new, ref_new, master_new.astype(jnp.bfloat16))

def add_piece(total, piece):
    return (total + piece.astype(jnp.float32), None)

def reference(text_grads, text_master, text_moment, text_second, text_ref, vision_grads, vision_master, vision_moment, vision_second, vision_ref):
    text_sum, _ = lax.scan(add_piece, jnp.zeros(text_master.shape, jnp.float32), text_grads)
    vision_sum, _ = lax.scan(add_piece, jnp.zeros(vision_master.shape, jnp.float32), vision_grads)
    text_out = adam_step(text_sum, text_moment, text_second, text_master, text_ref)
    vision_out = adam_step(vision_sum, vision_moment, vision_second, vision_master, vision_ref)
    return (text_out[0], text_out[1], text_out[2], text_out[3], text_out[4], vision_out[0], vision_out[1], vision_out[2], vision_out[3], vision_out[4])
```

```python
import functools

import jax
import jax.numpy as jnp
from jax import lax
from jax.experimental import pallas as pl
from jax.experimental.pallas import tpu as pltpu
from jax.sharding import PartitionSpec as P

MESH = pl.DeviceIdType.MESH
BF16, F32 = jnp.bfloat16, jnp.float32

beta_one = 0.9
beta_two = 0.95
correct_one = 1.0 - 0.9**10
correct_two = 1.0 - 0.95**10
learn_rate = 0.01
decay_rate = 0.1
blend_rate = 0.6

GROUPS = 16
ROWS = 80
COLS = 256
OPP, RIGHT, LEFT, REST, OWN = range(5)


def adam_step(grad, moment, second, master, refcopy):
    moment_new = beta_one * moment + (1.0 - beta_one) * grad
    second_new = beta_two * second + (1.0 - beta_two) * grad * grad
    update = moment_new / correct_one / (jnp.sqrt(second_new / correct_two) + 1e-08)
    master_new = master - learn_rate * (update + decay_rate * master)
    ref_new = blend_rate * master_new + (1.0 - blend_rate) * refcopy
    return (master_new, moment_new, second_new, ref_new, master_new.astype(BF16))


def place():
    dp, tensor = lax.axis_index("dp"), lax.axis_index("tensor")
    x = dp // 2
    z = (tensor // 8) * 2 + dp % 2
    y = (tensor % 8) // 2
    return x, y, z, tensor % 2


def device(x, y, z, core):
    return (x * 2 + z % 2, (z // 2) * 8 + y * 2 + core)


def group_of(x, z):
    return x * 4 + (z % 2) * 2 + z // 2


def plane_partner(x, z, k):
    return (x + k // 4) % 4, (z + k % 4) % 4


def line_partner(y, core, i):
    return (y + i // 2) % 4, (core + i % 2) % 2


def first_row(y):
    return pl.multiple_of(8 * ((5 * y) // 2), 8)


def remote(src, dst, send, recv, to):
    return pltpu.make_async_remote_copy(
        src_ref=src, dst_ref=dst, send_sem=send, recv_sem=recv, device_id=to, device_id_type=MESH
    )


def loop(first, last, step):
    def run(i, carry):
        step(i)
        return carry

    lax.fori_loop(first, last, run, 0)


def greet(x, y, z, core):
    barrier = pltpu.get_barrier_semaphore()

    def plane(k):
        px, pz = plane_partner(x, z, k)
        pl.semaphore_signal(barrier, inc=1, device_id=device(px, y, pz, core), device_id_type=MESH)

    def line(i):
        py, pc = line_partner(y, core, i)
        pl.semaphore_signal(barrier, inc=1, device_id=device(x, py, z, pc), device_id_type=MESH)

    loop(1, GROUPS, plane)
    loop(1, 8, line)
    pl.semaphore_wait(barrier, GROUPS - 1 + 7)


def scatter_kernel(
    text_hbm, vision_hbm, text_out, vision_out,
    mine, other, paired, over_a, over_b, from_left, from_right, total, plane_in, rest_in, rest_part, rest_line,
    sums, rest_sums, windows, text_own, text_in,
    load_sem, own_sem, pair_s, pair_r, y_s, y_r, plane_s, plane_r, rest_s, rest_r, rest_y_s, rest_y_r,
    win_s, win_r, text_s, text_r,
):
    x, y, z, core = place()
    dp = x * 2 + z % 2
    group = group_of(x, z)
    blocks = [(y + 2) % 4, (y + 1) % 4, (y + 3) % 4, 4, y]

    def loads(role):
        cols = pl.ds(pl.multiple_of(blocks[role] * COLS, COLS), COLS)
        return (
            pltpu.make_async_copy(vision_hbm.at[1 - core, :, :, cols], other.at[role], load_sem.at[role, 0]),
            pltpu.make_async_copy(vision_hbm.at[core, :, :, cols], mine.at[role], load_sem.at[role, 1]),
        )

    for role in (OPP, RIGHT, LEFT, REST, OWN):
        for copy in loads(role):
            copy.start()
    own_text = pltpu.make_async_copy(
        text_hbm.at[:, pl.ds(pl.multiple_of(dp * COLS, COLS), COLS)], text_own, own_sem
    )
    own_text.start()

    greet(x, y, z, core)

    def pair(role):
        return remote(other.at[role], paired.at[role], pair_s.at[role], pair_r.at[role], device(x, y, z, 1 - core))

    def text_copy(k):
        to = (dp + k) % 8
        return remote(
            text_hbm.at[:, pl.ds(pl.multiple_of(to * COLS, COLS), COLS)], text_in.at[k], text_s.at[k], text_r.at[k],
            (to, lax.axis_index("tensor")),
        )

    for role in (OPP, RIGHT, LEFT, REST, OWN):
        loads(role)[0].wait()
        pair(role).start()

    loop(1, 8, lambda k: text_copy(k).start())

    def add_pair(role):
        loads(role)[1].wait()
        pair(role).wait_recv()

        def add(g):
            mine[role, g] = mine[role, g] + paired[role, g]

        loop(0, GROUPS, add)

    right, left = device(x, (y + 1) % 4, z, core), device(x, (y + 3) % 4, z, core)
    half_a, half_b = pl.ds(0, 8), pl.ds(8, 8)
    along = [
        remote(mine.at[OPP, half_a], over_a, y_s.at[0], y_r.at[0], right),
        remote(mine.at[OPP, half_b], over_b, y_s.at[1], y_r.at[1], left),
        remote(mine.at[RIGHT, half_b], from_left.at[half_b], y_s.at[2], y_r.at[2], right),
        remote(mine.at[LEFT, half_a], from_right.at[half_a], y_s.at[3], y_r.at[3], left),
        remote(mine.at[RIGHT, half_a], from_left.at[half_a], y_s.at[4], y_r.at[4], right),
        remote(mine.at[LEFT, half_b], from_right.at[half_b], y_s.at[5], y_r.at[5], left),
    ]
    add_pair(OPP)
    along[0].start()
    along[1].start()
    add_pair(RIGHT)
    along[2].start()
    add_pair(LEFT)
    along[3].start()

    def rest_copy(k):
        px, pz = plane_partner(x, z, k)
        return remote(
            mine.at[REST, group_of(px, pz)], rest_in.at[k], rest_s.at[k], rest_r.at[k], device(px, y, pz, core)
        )

    add_pair(REST)
    loop(1, GROUPS, lambda k: rest_copy(k).start())
    add_pair(OWN)

    along[0].wait_recv()

    def add_a(g):
        mine[RIGHT, g] = mine[RIGHT, g] + over_a[g]

    loop(0, 8, add_a)
    along[4].start()
    along[1].wait_recv()

    def add_b(g):
        mine[LEFT, 8 + g] = mine[LEFT, 8 + g] + over_b[g]

    loop(0, 8, add_b)
    along[5].start()

    for copy in along[2:]:
        copy.wait_recv()

    def add_line(g):
        total[g] = (
            mine[OWN, g].astype(F32) + from_left[g].astype(F32) + from_right[g].astype(F32)
        ).astype(BF16)

    loop(0, GROUPS, add_line)

    def plane_copy(k):
        px, pz = plane_partner(x, z, k)
        return remote(total.at[group_of(px, pz)], plane_in.at[k], plane_s.at[k], plane_r.at[k], device(px, y, pz, core))

    loop(1, GROUPS, lambda k: plane_copy(k).start())

    loop(1, GROUPS, lambda k: rest_copy(k).wait_recv())
    acc = mine[REST, group].astype(F32)
    for k in range(1, GROUPS):
        acc = acc + rest_in[k].astype(F32)
    rest_part[...] = acc.astype(BF16)

    def rest_line_copy(k):
        return remote(
            rest_part, rest_line.at[k], rest_y_s.at[k], rest_y_r.at[k], device(x, (y + k) % 4, z, core)
        )

    for k in range(1, 4):
        rest_line_copy(k).start()

    own_text.wait()
    loop(1, 8, lambda k: text_copy(k).wait_recv())

    def add_text(i):
        rows = pl.ds(pl.multiple_of(i * 32, 32), 32)
        acc = text_own[rows].astype(F32)
        for k in range(1, 8):
            acc = acc + text_in[k, rows].astype(F32)
        text_out[rows] = acc

    loop(0, 16, add_text)

    for k in range(1, 4):
        rest_line_copy(k).wait_recv()
    acc = rest_part[...].astype(F32)
    for k in range(1, 4):
        acc = acc + rest_line[k].astype(F32)
    rest_sums[...] = acc
    own_rows = pl.ds(first_row(y), 24)
    windows[core, 4] = rest_sums[own_rows, :]
    rest_win = remote(
        rest_sums.at[own_rows], windows.at[core, 4], win_s.at[0], win_r.at[0], device(x, y, z, 1 - core)
    )
    rest_win.start()

    loop(1, GROUPS, lambda k: plane_copy(k).wait_recv())
    acc = total[group].astype(F32)
    for k in range(1, GROUPS):
        acc = acc + plane_in[k].astype(F32)
    sums[...] = acc

    def win_copy(i):
        py, pc = line_partner(y, core, i)
        return remote(
            sums.at[pl.ds(first_row(py), 24)], windows.at[core, y], win_s.at[i], win_r.at[i], device(x, py, z, pc)
        )

    loop(1, 8, lambda i: win_copy(i).start())
    windows[core, y] = sums[own_rows, :]

    for role in (OPP, RIGHT, LEFT, REST, OWN):
        pair(role).wait_send()
    for copy in along:
        copy.wait_send()
    loop(1, 8, lambda k: text_copy(k).wait_send())
    loop(1, GROUPS, lambda k: rest_copy(k).wait_send())
    loop(1, GROUPS, lambda k: plane_copy(k).wait_send())
    for k in range(1, 4):
        rest_line_copy(k).wait_send()
    rest_win.wait()
    loop(1, 8, lambda i: win_copy(i).wait())
    for layer in range(2):
        for block in range(5):
            vision_out[layer, :, block * COLS : (block + 1) * COLS] = windows[layer, block]


def scatter(text, vision):
    rows = text.shape[0]
    block = (GROUPS, ROWS, COLS)
    dma = pltpu.SemaphoreType.DMA
    return pl.pallas_call(
        scatter_kernel,
        name="sum_gradients",
        out_shape=(jax.ShapeDtypeStruct((rows, COLS), F32), jax.ShapeDtypeStruct((2, 24, 5 * COLS), F32)),
        in_specs=[pl.BlockSpec(memory_space=pltpu.HBM)] * 2,
        out_specs=[pl.BlockSpec(memory_space=pltpu.VMEM)] * 2,
        scratch_shapes=[
            pltpu.VMEM((5,) + block, BF16),
            pltpu.VMEM((5,) + block, BF16),
            pltpu.VMEM((5,) + block, BF16),
            pltpu.VMEM((8, ROWS, COLS), BF16),
            pltpu.VMEM((8, ROWS, COLS), BF16),
            pltpu.VMEM(block, BF16),
            pltpu.VMEM(block, BF16),
            pltpu.VMEM(block, BF16),
            pltpu.VMEM(block, BF16),
            pltpu.VMEM(block, BF16),
            pltpu.VMEM((ROWS, COLS), BF16),
            pltpu.VMEM((4, ROWS, COLS), BF16),
            pltpu.VMEM((ROWS, COLS), F32),
            pltpu.VMEM((ROWS, COLS), F32),
            pltpu.VMEM((2, 5, 24, COLS), F32),
            pltpu.VMEM((rows, COLS), BF16),
            pltpu.VMEM((8, rows, COLS), BF16),
            dma((5, 2)),
            dma,
            dma((5,)), dma((5,)),
            dma((6,)), dma((6,)),
            dma((GROUPS,)), dma((GROUPS,)),
            dma((GROUPS,)), dma((GROUPS,)),
            dma((4,)), dma((4,)),
            dma((8,)), dma((8,)),
            dma((8,)), dma((8,)),
        ],
        compiler_params=pltpu.CompilerParams(collective_id=1, has_side_effects=True, vmem_limit_bytes=40 << 20),
    )(text, vision)


def gather_kernel(
    text_w, vision_w, text_out, vision_out,
    staged, line_in, packed, blocks, from_pair,
    line_s, line_r, plane_s, plane_r, rest_s, rest_r, y_s, y_r, pair_s, pair_r, text_s, text_r, own_sem, out_sem,
):
    x, y, z, core = place()
    dp = x * 2 + z % 2
    group = group_of(x, z)
    cols_of = [(y + 2) % 4, (y + 1) % 4, (y + 3) % 4, 4, y]

    for layer in range(2):
        for block in range(4):
            staged[layer, block, :, :COLS] = vision_w[layer, :, block * COLS : (block + 1) * COLS]
            staged[layer, block, :, COLS:] = vision_w[layer, :, 4 * COLS :]

    greet(x, y, z, core)

    def line_copy(i):
        py, pc = line_partner(y, core, i)
        return remote(
            staged.at[pc, py], line_in.at[y * 2 + core], line_s.at[i], line_r.at[i], device(x, py, z, pc)
        )

    loop(1, 8, lambda i: line_copy(i).start())
    line_in[y * 2 + core] = staged[core, y]

    loop(1, 8, lambda i: line_copy(i).wait_recv())
    for i in range(8):
        packed[10 * i : 10 * i + 10, :] = line_in[i].astype(F32)[:10]
    blocks[OWN, group] = packed[:, :COLS].astype(BF16)
    blocks[REST, group] = packed[:, COLS:].astype(BF16)

    def plane_copy(k):
        px, pz = plane_partner(x, z, k)
        return remote(
            blocks.at[OWN, group], blocks.at[OWN, group], plane_s.at[k], plane_r.at[k], device(px, y, pz, core)
        )

    def rest_copy(k):
        px, pz = plane_partner(x, z, k)
        return remote(
            blocks.at[REST, group], blocks.at[REST, group], rest_s.at[k], rest_r.at[k], device(px, y, pz, core)
        )

    def text_cols(k):
        return text_out.at[:, pl.ds(pl.multiple_of(k * COLS, COLS), COLS)]

    def text_copy(k):
        return remote(text_w, text_cols(dp), text_s.at[k], text_r.at[k], ((dp + k) % 8, lax.axis_index("tensor")))

    loop(1, GROUPS, lambda k: plane_copy(k).start())
    own_text = pltpu.make_async_copy(text_w, text_cols(dp), own_sem)
    own_text.start()
    loop(1, 8, lambda k: text_copy(k).start())
    loop(1, GROUPS, lambda k: rest_copy(k).start())

    def pair(role):
        return remote(blocks.at[role], from_pair.at[role], pair_s.at[role], pair_r.at[role], device(x, y, z, 1 - core))

    def writes(role):
        cols = pl.ds(pl.multiple_of(cols_of[role] * COLS, COLS), COLS)
        return (
            pltpu.make_async_copy(blocks.at[role], vision_out.at[core, :, :, cols], out_sem.at[role, 0]),
            pltpu.make_async_copy(from_pair.at[role], vision_out.at[1 - core, :, :, cols], out_sem.at[role, 1]),
        )

    right, left = device(x, (y + 1) % 4, z, core), device(x, (y + 3) % 4, z, core)
    half_a, half_b = pl.ds(0, 8), pl.ds(8, 8)
    along = [
        remote(blocks.at[OWN, half_a], blocks.at[LEFT, half_a], y_s.at[0], y_r.at[0], right),
        remote(blocks.at[OWN, half_b], blocks.at[RIGHT, half_b], y_s.at[1], y_r.at[1], left),
        remote(blocks.at[OWN, half_b], blocks.at[LEFT, half_b], y_s.at[2], y_r.at[2], right),
        remote(blocks.at[OWN, half_a], blocks.at[RIGHT, half_a], y_s.at[3], y_r.at[3], left),
        remote(blocks.at[LEFT, half_a], blocks.at[OPP, half_a], y_s.at[4], y_r.at[4], right),
        remote(blocks.at[RIGHT, half_b], blocks.at[OPP, half_b], y_s.at[5], y_r.at[5], left),
    ]

    loop(1, GROUPS, lambda k: plane_copy(k).wait_recv())
    for copy in along[:4]:
        copy.start()
    pair(OWN).start()
    writes(OWN)[0].start()
    along[0].wait_recv()
    along[4].start()
    along[1].wait_recv()
    along[5].start()
    along[2].wait_recv()
    pair(LEFT).start()
    writes(LEFT)[0].start()
    along[3].wait_recv()
    pair(RIGHT).start()
    writes(RIGHT)[0].start()
    pair(OWN).wait_recv()
    writes(OWN)[1].start()
    loop(1, GROUPS, lambda k: rest_copy(k).wait_recv())
    pair(REST).start()
    writes(REST)[0].start()
    along[4].wait_recv()
    along[5].wait_recv()
    pair(OPP).start()
    writes(OPP)[0].start()
    for role in (LEFT, RIGHT, REST, OPP):
        pair(role).wait_recv()
        writes(role)[1].start()

    loop(1, 8, lambda i: line_copy(i).wait_send())
    loop(1, GROUPS, lambda k: plane_copy(k).wait_send())
    loop(1, GROUPS, lambda k: rest_copy(k).wait_send())
    own_text.wait()
    loop(1, 8, lambda k: text_copy(k).wait())
    for copy in along:
        copy.wait_send()
    for role in (OWN, LEFT, RIGHT, REST, OPP):
        pair(role).wait_send()
        for copy in writes(role):
            copy.wait()


def gather(text_w, vision_w):
    rows = text_w.shape[0]
    block = (GROUPS, ROWS, COLS)
    dma = pltpu.SemaphoreType.DMA
    return pl.pallas_call(
        gather_kernel,
        name="gather_weights",
        out_shape=(
            jax.ShapeDtypeStruct((rows, 8 * COLS), BF16),
            jax.ShapeDtypeStruct((2, GROUPS, ROWS, 5 * COLS), BF16),
        ),
        in_specs=[pl.BlockSpec(memory_space=pltpu.VMEM)] * 2,
        out_specs=[pl.BlockSpec(memory_space=pltpu.HBM)] * 2,
        scratch_shapes=[
            pltpu.VMEM((2, 4, 16, 2 * COLS), BF16),
            pltpu.VMEM((8, 16, 2 * COLS), BF16),
            pltpu.VMEM((ROWS, 2 * COLS), F32),
            pltpu.VMEM((5,) + block, BF16),
            pltpu.VMEM((5,) + block, BF16),
            dma((8,)), dma((8,)),
            dma((GROUPS,)), dma((GROUPS,)),
            dma((GROUPS,)), dma((GROUPS,)),
            dma((6,)), dma((6,)),
            dma((5,)), dma((5,)),
            dma((8,)), dma((8,)),
            dma,
            dma((5, 2)),
        ],
        compiler_params=pltpu.CompilerParams(collective_id=2, has_side_effects=True, vmem_limit_bytes=40 << 20),
    )(text_w, vision_w)


def body(
    text_grads, text_master, text_moment, text_second, text_ref,
    vision_grads, vision_master, vision_moment, vision_second, vision_ref,
):
    layers, width = vision_grads.shape[1], vision_grads.shape[3]
    text_total, windows = scatter(text_grads[0], vision_grads.reshape(layers, GROUPS, ROWS, width))
    _, y, _, core = place()
    first = 20 * y + 10 * core - 8 * ((5 * y) // 2)
    vision_total = lax.dynamic_slice_in_dim(windows, first, 10, axis=1)
    text_out = adam_step(text_total, text_moment, text_second, text_master, text_ref)
    vision_out = adam_step(vision_total, vision_moment, vision_second, vision_master, vision_ref)
    vision_padded = jnp.pad(vision_out[4], ((0, 0), (0, 6), (0, 0)))
    text_full, vision_full = gather(text_out[4], vision_padded)
    return text_out[:4] + (text_full,) + vision_out[:4] + (vision_full.reshape(layers, width, width),)


def solution(mesh):
    owned = P("tensor", "dp")
    vision_owned = P(None, ("dp", "tensor"), None)
    return jax.shard_map(
        body,
        mesh=mesh,
        in_specs=(P("dp", "tensor", None),) + (owned,) * 4 + (P(("dp", "tensor"), None, None, None),) + (vision_owned,) * 4,
        out_specs=(owned,) * 4 + (P("tensor", None),) + (vision_owned,) * 4 + (P(),),
        check_vma=False,
    )
```

```python
import functools

import jax
import jax.numpy as jnp
from jax import lax
from jax.experimental import pallas as pl
from jax.experimental.pallas import tpu as pltpu
from jax.sharding import PartitionSpec as P

MESH = pl.DeviceIdType.MESH
BF16, F32 = jnp.bfloat16, jnp.float32

beta_one = 0.9
beta_two = 0.95
correct_one = 1.0 - 0.9**10
correct_two = 1.0 - 0.95**10
learn_rate = 0.01
decay_rate = 0.1
blend_rate = 0.6

GROUPS = 16
ROWS = 80
TILE = 128
COLS = 2 * TILE
OPP, RIGHT, LEFT, OWN, REST = range(5)
REST_0, REST_1, MAIN_0, MAIN_1 = range(4)


def adam_step(grad, moment, second, master, refcopy):
    moment_new = beta_one * moment + (1.0 - beta_one) * grad
    second_new = beta_two * second + (1.0 - beta_two) * grad * grad
    update = moment_new / correct_one / (jnp.sqrt(second_new / correct_two) + 1e-08)
    master_new = master - learn_rate * (update + decay_rate * master)
    ref_new = blend_rate * master_new + (1.0 - blend_rate) * refcopy
    return (master_new, moment_new, second_new, ref_new, master_new.astype(BF16))


def place():
    dp, tensor = lax.axis_index("dp"), lax.axis_index("tensor")
    x = dp // 2
    z = (tensor // 8) * 2 + dp % 2
    y = (tensor % 8) // 2
    return x, y, z, tensor % 2


def device(x, y, z, core):
    return (x * 2 + z % 2, (z // 2) * 8 + y * 2 + core)


def group_of(x, z):
    return x * 4 + (z % 2) * 2 + z // 2


def first_row(y):
    return pl.multiple_of(8 * ((5 * y) // 2), 8)


def columns(block, width):
    return pl.ds(pl.multiple_of(block * width, width), width)


def remote(src, dst, send, recv, to):
    return pltpu.make_async_remote_copy(
        src_ref=src, dst_ref=dst, send_sem=send, recv_sem=recv, device_id=to, device_id_type=MESH
    )


def loop(first, last, step):
    def run(i, carry):
        step(i)
        return carry

    lax.fori_loop(first, last, run, 0)


class Near:
    def __init__(self):
        self.x, self.y, self.z, self.core = place()
        x, y, z, core = self.x, self.y, self.z, self.core
        self.dp = x * 2 + z % 2
        self.twin = z % 2
        self.a = x * (1 - core) + z * core
        self.b = x * core + z * (1 - core)
        self.right = device(x, (y + 1) % 4, z, core)
        self.left = device(x, (y + 3) % 4, z, core)
        self.mate = device(x, y, z, 1 - core)
        self.beside = device(x, y, z + 1 - 2 * (z % 2), core)

    def along_a(self, k):
        core = self.core
        return device((self.x + k * (1 - core)) % 4, self.y, (self.z + k * core) % 4, core)

    def along_b(self, k):
        core = self.core
        return device((self.x + k * core) % 4, self.y, (self.z + k * (1 - core)) % 4, core)

    def along_x(self, k):
        return device((self.x + k) % 4, self.y, self.z, self.core)

    def line(self, i):
        py, pc = (self.y + i // 2) % 4, (self.core + i % 2) % 2
        return device(self.x, py, self.z, pc), py, pc

    def group(self, a, b):
        core = self.core
        return group_of(a * (1 - core) + b * core, a * core + b * (1 - core))

    def greet(self):
        barrier = pltpu.get_barrier_semaphore()

        def signal(to):
            pl.semaphore_signal(barrier, inc=1, device_id=to, device_id_type=MESH)

        loop(1, 4, lambda k: signal(self.along_a(k)))
        loop(1, 4, lambda k: signal(self.along_b(k)))
        loop(1, 8, lambda i: signal(self.line(i)[0]))
        pl.semaphore_wait(barrier, 13)


def scatter_kernel(
    text_hbm, vision_hbm, text_out, vision_out,
    mine, other, paired, main, rest, over_a, over_b, from_left, from_right, total, first_in, first_sum, second_in,
    rest_part, rest_line, sums, rest_sums, windows, upper, lower_own, lower_in, lower_sum, cross_out, cross_in, lower_x,
    load_sem, text_load, pair_s, pair_r, y_s, y_r, first_s, first_r, second_s, second_r, rest_y_s, rest_y_r,
    win_s, win_r, text_s, text_r, text2_s, text2_r,
):
    near = Near()
    x, y, core = near.x, near.y, near.core
    half_rows = text_hbm.shape[0] // 2
    blocks = [(y + 2) % 4, (y + 1) % 4, (y + 3) % 4, y, 4]
    order = (OPP, RIGHT, LEFT, REST, OWN)

    def loads(role):
        cols = columns(blocks[role], COLS)
        return (
            pltpu.make_async_copy(vision_hbm.at[1 - core, :, :, cols], other.at[role], load_sem.at[role, 0]),
            pltpu.make_async_copy(vision_hbm.at[core, :, :, cols], mine.at[role], load_sem.at[role, 1]),
        )

    def text_block(half, block):
        return text_hbm.at[pl.ds(half * half_rows, half_rows), columns(block, COLS)]

    def upper_load(q):
        return pltpu.make_async_copy(text_block(0, 2 * x + q), upper.at[0, q], text_load.at[q])

    def lower_load(px):
        return pltpu.make_async_copy(text_block(1, 2 * px + near.twin), lower_own.at[px], text_load.at[2 + px])

    for role in order:
        for copy in loads(role):
            copy.start()
    loop(0, 2, lambda q: upper_load(q).start())
    loop(0, 4, lambda px: lower_load(px).start())

    near.greet()

    def upper_copy(k, q):
        to = (x + k) % 4
        return remote(
            text_block(0, 2 * to + q), upper.at[k, q], text_s.at[k, q], text_r.at[k, q], near.along_x(k)
        )

    def lower_copy(px):
        return remote(
            text_block(1, 2 * px + 1 - near.twin), lower_in.at[px], text_s.at[4 + px, 0], text_r.at[4 + px, 0],
            near.beside,
        )

    def pair(role):
        return remote(other.at[role], paired.at[role], pair_s.at[role], pair_r.at[role], near.mate)

    for role in order:
        loads(role)[0].wait()
        pair(role).start()

    for k in range(1, 4):
        for q in range(2):
            upper_copy(k, q).start()
    loop(0, 4, lambda px: lower_copy(px).start())

    def ready(role):
        loads(role)[1].wait()
        pair(role).wait_recv()

    def add_pair(role):
        ready(role)

        def add(g):
            both = mine[role, g] + paired[role, g]
            main[role, 0, g] = both[:, :TILE]
            main[role, 1, g] = both[:, TILE:]

        loop(0, GROUPS, add)

    def add_rest():
        ready(REST)

        def add(i):
            a, b = i // 4, i % 4
            g = near.group(a, b)
            both = mine[REST, g] + paired[REST, g]
            rest[0, a, b] = both[:, :TILE]
            rest[1, a, b] = both[:, TILE:]

        loop(0, GROUPS, add)

    half_a, half_b = pl.ds(0, 8), pl.ds(8, 8)

    def along(tile):
        def go(src, dst, i, to):
            return remote(src, dst, y_s.at[tile, i], y_r.at[tile, i], to)

        return [
            go(main.at[OPP, tile, half_a], over_a.at[tile], 0, near.right),
            go(main.at[OPP, tile, half_b], over_b.at[tile], 1, near.left),
            go(main.at[RIGHT, tile, half_b], from_left.at[tile, half_b], 2, near.right),
            go(main.at[LEFT, tile, half_a], from_right.at[tile, half_a], 3, near.left),
            go(main.at[RIGHT, tile, half_a], from_left.at[tile, half_a], 4, near.right),
            go(main.at[LEFT, tile, half_b], from_right.at[tile, half_b], 5, near.left),
        ]

    line = [along(0), along(1)]

    def pass_on(tile):
        line[tile][0].wait_recv()

        def add_a(g):
            main[RIGHT, tile, g] = main[RIGHT, tile, g] + over_a[tile, g]

        loop(0, 8, add_a)
        line[tile][4].start()
        line[tile][1].wait_recv()

        def add_b(g):
            main[LEFT, tile, 8 + g] = main[LEFT, tile, 8 + g] + over_b[tile, g]

        loop(0, 8, add_b)
        line[tile][5].start()

    def add_line(tile):
        for copy in line[tile][2:]:
            copy.wait_recv()

        def add(i):
            a, b = i // 4, i % 4
            g = near.group(a, b)
            total[tile, a, b] = (
                main[OWN, tile, g].astype(F32) + from_left[tile, g].astype(F32) + from_right[tile, g].astype(F32)
            ).astype(BF16)

        loop(0, GROUPS, add)

    def source(part):
        return rest.at[part] if part < MAIN_0 else total.at[part - MAIN_0]

    def first_copy(part, k):
        return remote(
            source(part).at[(near.a + k) % 4], first_in.at[part, k], first_s.at[part, k], first_r.at[part, k],
            near.along_a(k),
        )

    def second_copy(part, k):
        return remote(
            first_sum.at[part, (near.b + k) % 4], second_in.at[part, k], second_s.at[part, k], second_r.at[part, k],
            near.along_b(k),
        )

    def first_step(part):
        loop(1, 4, lambda k: first_copy(part, k).start())

    def second_step(part):
        loop(1, 4, lambda k: first_copy(part, k).wait_recv())
        own = source(part).at[near.a]

        def add(b):
            acc = own[b].astype(F32)
            for k in range(1, 4):
                acc = acc + first_in[part, k, b].astype(F32)
            first_sum[part, b] = acc.astype(BF16)

        loop(0, 4, add)
        loop(1, 4, lambda k: second_copy(part, k).start())

    def last_step(part):
        loop(1, 4, lambda k: second_copy(part, k).wait_recv())
        acc = first_sum[part, near.b].astype(F32)
        for k in range(1, 4):
            acc = acc + second_in[part, k].astype(F32)
        return acc

    add_pair(OPP)
    line[0][0].start()
    line[0][1].start()
    add_pair(RIGHT)
    line[0][2].start()
    add_pair(LEFT)
    line[0][3].start()
    add_rest()
    first_step(REST_0)
    first_step(REST_1)
    add_pair(OWN)
    pass_on(0)
    for copy in line[1][:4]:
        copy.start()
    second_step(REST_0)
    second_step(REST_1)

    def cross_copy():
        return remote(cross_out, cross_in, text2_s.at[0], text2_r.at[0], near.beside)

    def lower_x_copy(k):
        return remote(
            lower_sum.at[(x + k) % 4], lower_x.at[k], text2_s.at[k], text2_r.at[k], near.along_x(k)
        )

    def text_middle():
        loop(0, 2, lambda q: upper_load(q).wait())
        for k in range(1, 4):
            for q in range(2):
                upper_copy(k, q).wait_recv()

        def add_upper(i):
            rows = pl.ds(pl.multiple_of(i * 32, 32), 32)
            acc_out = upper[0, 1 - near.twin, rows].astype(F32)
            acc_own = upper[0, near.twin, rows].astype(F32)
            for k in range(1, 4):
                acc_out = acc_out + upper[k, 1 - near.twin, rows].astype(F32)
                acc_own = acc_own + upper[k, near.twin, rows].astype(F32)
            cross_out[rows] = acc_out.astype(BF16)
            text_out[rows] = acc_own

        loop(0, half_rows // 32, add_upper)
        cross_copy().start()
        loop(0, 4, lambda px: lower_load(px).wait())
        loop(0, 4, lambda px: lower_copy(px).wait_recv())

        def add_lower(i):
            px, rows = i // 4, pl.ds(pl.multiple_of((i % 4) * 64, 64), 64)
            lower_sum[px, rows] = lower_own[px, rows] + lower_in[px, rows]

        loop(0, half_rows // 16, add_lower)
        loop(1, 4, lambda k: lower_x_copy(k).start())

    def text_last():
        cross_copy().wait_recv()
        loop(1, 4, lambda k: lower_x_copy(k).wait_recv())

        def add(i):
            rows = pl.ds(pl.multiple_of(i * 32, 32), 32)
            text_out[rows] = text_out[rows] + cross_in[rows].astype(F32)
            acc = lower_own[x, rows].astype(F32) + lower_in[x, rows].astype(F32)
            for k in range(1, 4):
                acc = acc + lower_x[k, rows].astype(F32)
            text_out[pl.ds(pl.multiple_of(half_rows + i * 32, 32), 32)] = acc

        loop(0, half_rows // 32, add)

    def rest_line_copy(k):
        return remote(
            rest_part, rest_line.at[k], rest_y_s.at[k], rest_y_r.at[k], device(x, (y + k) % 4, near.z, core)
        )

    own_rows = pl.ds(first_row(y), 24)

    def rest_win():
        return remote(
            rest_sums.at[:, own_rows], windows.at[core, pl.ds(8, 2)], win_s.at[0, 0], win_r.at[0, 0], near.mate
        )

    def win_copy(tile, i):
        to, py, _ = near.line(i)
        return remote(
            sums.at[tile, pl.ds(first_row(py), 24)], windows.at[core, 2 * y + tile], win_s.at[tile, i], win_r.at[tile, i],
            to,
        )

    def main_last(tile):
        sums[tile] = last_step(MAIN_0 + tile)
        loop(1, 8, lambda i: win_copy(tile, i).start())
        windows[core, 2 * y + tile] = sums[tile, own_rows]

    add_line(0)
    first_step(MAIN_0)
    pass_on(1)
    text_middle()
    for tile in range(2):
        rest_part[tile] = last_step(REST_0 + tile).astype(BF16)
    loop(1, 4, lambda k: rest_line_copy(k).start())
    second_step(MAIN_0)
    add_line(1)
    first_step(MAIN_1)

    loop(1, 4, lambda k: rest_line_copy(k).wait_recv())
    for tile in range(2):
        acc = rest_part[tile].astype(F32)
        for k in range(1, 4):
            acc = acc + rest_line[k, tile].astype(F32)
        rest_sums[tile] = acc
        windows[core, 8 + tile] = rest_sums[tile, own_rows]
    rest_win().start()
    main_last(0)
    second_step(MAIN_1)
    text_last()
    main_last(1)

    for role in order:
        pair(role).wait_send()
    for copy in line[0] + line[1]:
        copy.wait_send()
    for k in range(1, 4):
        for q in range(2):
            upper_copy(k, q).wait_send()
    loop(0, 4, lambda px: lower_copy(px).wait_send())
    cross_copy().wait_send()
    loop(1, 4, lambda k: lower_x_copy(k).wait_send())
    for part in range(4):
        loop(1, 4, lambda k: first_copy(part, k).wait_send())
        loop(1, 4, lambda k: second_copy(part, k).wait_send())
    loop(1, 4, lambda k: rest_line_copy(k).wait_send())
    rest_win().wait()
    for tile in range(2):
        loop(1, 8, lambda i: win_copy(tile, i).wait())
    for layer in range(2):
        for t in range(10):
            vision_out[layer, :, t * TILE : (t + 1) * TILE] = windows[layer, t]


def scatter(text, vision):
    rows = text.shape[0]
    half = rows // 2
    block = (GROUPS, ROWS, COLS)
    tile = (GROUPS, ROWS, TILE)
    plane = (4, 4, ROWS, TILE)
    dma = pltpu.SemaphoreType.DMA
    return pl.pallas_call(
        scatter_kernel,
        name="sum_gradients",
        out_shape=(jax.ShapeDtypeStruct((rows, COLS), F32), jax.ShapeDtypeStruct((2, 24, 5 * COLS), F32)),
        in_specs=[pl.BlockSpec(memory_space=pltpu.HBM)] * 2,
        out_specs=[pl.BlockSpec(memory_space=pltpu.VMEM)] * 2,
        scratch_shapes=[
            pltpu.VMEM((5,) + block, BF16),
            pltpu.VMEM((5,) + block, BF16),
            pltpu.VMEM((5,) + block, BF16),
            pltpu.VMEM((4, 2) + tile, BF16),
            pltpu.VMEM((2,) + plane, BF16),
            pltpu.VMEM((2, 8, ROWS, TILE), BF16),
            pltpu.VMEM((2, 8, ROWS, TILE), BF16),
            pltpu.VMEM((2,) + tile, BF16),
            pltpu.VMEM((2,) + tile, BF16),
            pltpu.VMEM((2,) + plane, BF16),
            pltpu.VMEM((4,) + plane, BF16),
            pltpu.VMEM((4, 4, ROWS, TILE), BF16),
            pltpu.VMEM((4, 4, ROWS, TILE), BF16),
            pltpu.VMEM((2, ROWS, TILE), BF16),
            pltpu.VMEM((4, 2, ROWS, TILE), BF16),
            pltpu.VMEM((2, ROWS, TILE), F32),
            pltpu.VMEM((2, ROWS, TILE), F32),
            pltpu.VMEM((2, 10, 24, TILE), F32),
            pltpu.VMEM((4, 2, half, COLS), BF16),
            pltpu.VMEM((4, half, COLS), BF16),
            pltpu.VMEM((4, half, COLS), BF16),
            pltpu.VMEM((4, half, COLS), BF16),
            pltpu.VMEM((half, COLS), BF16),
            pltpu.VMEM((half, COLS), BF16),
            pltpu.VMEM((4, half, COLS), BF16),
            dma((5, 2)),
            dma((6,)),
            dma((5,)), dma((5,)),
            dma((2, 6)), dma((2, 6)),
            dma((4, 4)), dma((4, 4)),
            dma((4, 4)), dma((4, 4)),
            dma((4,)), dma((4,)),
            dma((2, 8)), dma((2, 8)),
            dma((8, 2)), dma((8, 2)),
            dma((4,)), dma((4,)),
        ],
        compiler_params=pltpu.CompilerParams(collective_id=1, has_side_effects=True, vmem_limit_bytes=SCATTER_VMEM),
    )(text, vision)


SCATTER_VMEM = 56 << 20


def gather_kernel(
    text_w, vision_w, text_out, vision_out,
    staged, line_in, packed, plane, main, rest, from_pair,
    line_s, line_r, first_s, first_r, second_s, second_r, y_s, y_r, pair_s, pair_r, text_s, text_r, own_sem, out_sem,
):
    near = Near()
    x, y, core = near.x, near.y, near.core
    half_rows = text_w.shape[0] // 2
    upper, lower = pl.ds(0, half_rows), pl.ds(half_rows, half_rows)

    for layer in range(2):
        for block in range(4):
            staged[layer, block, :, :COLS] = vision_w[layer, :, block * COLS : (block + 1) * COLS]
            staged[layer, block, :, COLS:] = vision_w[layer, :, 4 * COLS :]

    near.greet()

    def line_copy(i):
        to, py, pc = near.line(i)
        return remote(staged.at[pc, py], line_in.at[y * 2 + core], line_s.at[i], line_r.at[i], to)

    own_cols = columns(near.dp, COLS)

    def own_text():
        return pltpu.make_async_copy(text_w, text_out.at[:, own_cols], own_sem)

    def beside_copy():
        return remote(text_w.at[upper], text_out.at[upper, own_cols], text_s.at[0, 0], text_r.at[0, 0], near.beside)

    def x_copy(k):
        return remote(text_w.at[lower], text_out.at[lower, own_cols], text_s.at[0, k], text_r.at[0, k], near.along_x(k))

    def upper_copy(k):
        both = text_out.at[upper, columns(x, 2 * COLS)]
        return remote(both, both, text_s.at[1, k], text_r.at[1, k], near.along_x(k))

    def lower_copy(px):
        one = text_out.at[lower, columns(2 * px + near.twin, COLS)]
        return remote(one, one, text_s.at[2, px], text_r.at[2, px], near.beside)

    loop(1, 8, lambda i: line_copy(i).start())
    own_text().start()
    beside_copy().start()
    loop(1, 4, lambda k: x_copy(k).start())
    line_in[y * 2 + core] = staged[core, y]
    loop(1, 8, lambda i: line_copy(i).wait_recv())
    for i in range(8):
        packed[10 * i : 10 * i + 10, :] = line_in[i].astype(F32)[:10]
    for part, first in ((MAIN_0, 0), (MAIN_1, 1), (REST_0, 2), (REST_1, 3)):
        plane[part, near.a, near.b] = packed[:, first * TILE : (first + 1) * TILE].astype(BF16)

    def first_copy(part, k):
        one = plane.at[part, near.a, near.b]
        return remote(one, one, first_s.at[part, k], first_r.at[part, k], near.along_b(k))

    def second_copy(part, k):
        row = plane.at[part, near.a]
        return remote(row, row, second_s.at[part, k], second_r.at[part, k], near.along_a(k))

    parts = (MAIN_0, MAIN_1, REST_0, REST_1)
    for part in parts:
        loop(1, 4, lambda k: first_copy(part, k).start())
    for part in parts:
        loop(1, 4, lambda k: first_copy(part, k).wait_recv())
        loop(1, 4, lambda k: second_copy(part, k).start())

    def spread(part, dst):
        loop(1, 4, lambda k: second_copy(part, k).wait_recv())

        def move(i):
            a, b = i // 4, i % 4
            dst[near.group(a, b)] = plane[part, a, b]

        loop(0, GROUPS, move)

    half_a, half_b = pl.ds(0, 8), pl.ds(8, 8)

    def along(tile):
        def go(src, dst, half, i, to):
            return remote(main.at[src, tile, half], main.at[dst, tile, half], y_s.at[tile, i], y_r.at[tile, i], to)

        return [
            go(OWN, LEFT, half_a, 0, near.right),
            go(OWN, RIGHT, half_b, 1, near.left),
            go(OWN, LEFT, half_b, 2, near.right),
            go(OWN, RIGHT, half_a, 3, near.left),
            go(LEFT, OPP, half_a, 4, near.right),
            go(RIGHT, OPP, half_b, 5, near.left),
        ]

    line = [along(0), along(1)]
    tiles = {OPP: 2 * ((y + 2) % 4), RIGHT: 2 * ((y + 1) % 4), LEFT: 2 * ((y + 3) % 4), OWN: 2 * y, REST: 8}

    def held(role, tile):
        return rest.at[tile] if role == REST else main.at[role, tile]

    def pair(role, tile):
        return remote(
            held(role, tile), from_pair.at[role, tile], pair_s.at[role, tile], pair_r.at[role, tile], near.mate
        )

    def write(role, tile, which):
        src = from_pair.at[role, tile] if which else held(role, tile)
        layer = 1 - core if which else core
        cols = columns(tiles[role] + tile, TILE)
        return pltpu.make_async_copy(src, vision_out.at[layer, :, :, cols], out_sem.at[role, tile, which])

    def give(role, tile):
        pair(role, tile).start()
        write(role, tile, 0).start()

    spread(MAIN_0, main.at[OWN, 0])
    for copy in line[0][:4]:
        copy.start()
    spread(MAIN_1, main.at[OWN, 1])
    give(OWN, 0)
    give(OWN, 1)

    own_text().wait()
    beside_copy().wait_recv()
    loop(1, 4, lambda k: upper_copy(k).start())
    loop(1, 4, lambda k: x_copy(k).wait_recv())
    loop(0, 4, lambda px: lower_copy(px).start())

    line[0][0].wait_recv()
    line[0][4].start()
    line[0][1].wait_recv()
    line[0][5].start()
    for copy in line[1][:4]:
        copy.start()

    for tile in range(2):
        spread(REST_0 + tile, rest.at[tile])
        give(REST, tile)
    for tile in range(2):
        line[tile][2].wait_recv()
        give(LEFT, tile)
        line[tile][3].wait_recv()
        give(RIGHT, tile)
        if tile == 0:
            line[1][0].wait_recv()
            line[1][4].start()
            line[1][1].wait_recv()
            line[1][5].start()
        line[tile][4].wait_recv()
        line[tile][5].wait_recv()
        give(OPP, tile)

    arrivals = [(OWN, 0), (OWN, 1), (REST, 0), (REST, 1), (LEFT, 0), (RIGHT, 0), (OPP, 0), (LEFT, 1), (RIGHT, 1), (OPP, 1)]
    loop(1, 8, lambda i: line_copy(i).wait_send())
    for part in parts:
        loop(1, 4, lambda k: first_copy(part, k).wait_send())
        loop(1, 4, lambda k: second_copy(part, k).wait_send())
    beside_copy().wait_send()
    loop(1, 4, lambda k: x_copy(k).wait_send())
    loop(1, 4, lambda k: upper_copy(k).wait())
    loop(0, 4, lambda px: lower_copy(px).wait())
    for role, tile in arrivals:
        pair(role, tile).wait_recv()
        write(role, tile, 1).start()
    for copy in line[0] + line[1]:
        copy.wait_send()
    for role, tile in arrivals:
        pair(role, tile).wait_send()
        write(role, tile, 0).wait()
        write(role, tile, 1).wait()


def gather(text_w, vision_w):
    rows = text_w.shape[0]
    tile = (GROUPS, ROWS, TILE)
    dma = pltpu.SemaphoreType.DMA
    return pl.pallas_call(
        gather_kernel,
        name="gather_weights",
        out_shape=(
            jax.ShapeDtypeStruct((rows, 8 * COLS), BF16),
            jax.ShapeDtypeStruct((2, GROUPS, ROWS, 5 * COLS), BF16),
        ),
        in_specs=[pl.BlockSpec(memory_space=pltpu.VMEM)] * 2,
        out_specs=[pl.BlockSpec(memory_space=pltpu.HBM)] * 2,
        scratch_shapes=[
            pltpu.VMEM((2, 4, 16, 2 * COLS), BF16),
            pltpu.VMEM((8, 16, 2 * COLS), BF16),
            pltpu.VMEM((ROWS, 2 * COLS), F32),
            pltpu.VMEM((4, 4, 4, ROWS, TILE), BF16),
            pltpu.VMEM((4, 2) + tile, BF16),
            pltpu.VMEM((2,) + tile, BF16),
            pltpu.VMEM((5, 2) + tile, BF16),
            dma((8,)), dma((8,)),
            dma((4, 4)), dma((4, 4)),
            dma((4, 4)), dma((4, 4)),
            dma((2, 6)), dma((2, 6)),
            dma((5, 2)), dma((5, 2)),
            dma((3, 4)), dma((3, 4)),
            dma,
            dma((5, 2, 2)),
        ],
        compiler_params=pltpu.CompilerParams(collective_id=2, has_side_effects=True, vmem_limit_bytes=24 << 20),
    )(text_w, vision_w)


def body(
    text_grads, text_master, text_moment, text_second, text_ref,
    vision_grads, vision_master, vision_moment, vision_second, vision_ref,
):
    layers, width = vision_grads.shape[1], vision_grads.shape[3]
    text_total, windows = scatter(text_grads[0], vision_grads.reshape(layers, GROUPS, ROWS, width))
    _, y, _, core = place()
    first = 20 * y + 10 * core - 8 * ((5 * y) // 2)
    vision_total = lax.dynamic_slice_in_dim(windows, first, 10, axis=1)
    text_out = adam_step(text_total, text_moment, text_second, text_master, text_ref)

    def rows_first(array):
        return jnp.transpose(array, (1, 0, 2))

    vision_out = adam_step(*map(rows_first, (vision_total, vision_moment, vision_second, vision_master, vision_ref)))
    vision_out = tuple(map(rows_first, vision_out))
    vision_padded = jnp.pad(vision_out[4], ((0, 0), (0, 6), (0, 0)))
    text_full, vision_full = gather(text_out[4], vision_padded)
    return text_out[:4] + (text_full,) + vision_out[:4] + (vision_full.reshape(layers, width, width),)


def solution(mesh):
    owned = P("tensor", "dp")
    vision_owned = P(None, ("dp", "tensor"), None)
    return jax.shard_map(
        body,
        mesh=mesh,
        in_specs=(P("dp", "tensor", None),) + (owned,) * 4 + (P(("dp", "tensor"), None, None, None),) + (vision_owned,) * 4,
        out_specs=(owned,) * 4 + (P("tensor", None),) + (vision_owned,) * 4 + (P(),),
        check_vma=False,
    )
```

```python
import functools

import jax
import jax.numpy as jnp
from jax import lax
from jax.experimental import pallas as pl
from jax.experimental.pallas import tpu as pltpu
from jax.sharding import PartitionSpec as P

MESH = pl.DeviceIdType.MESH
BF16, F32 = jnp.bfloat16, jnp.float32

beta_one = 0.9
beta_two = 0.95
correct_one = 1.0 - 0.9**10
correct_two = 1.0 - 0.95**10
learn_rate = 0.01
decay_rate = 0.1
blend_rate = 0.6

GROUPS = 16
ROWS = 80
TILE = 128
COLS = 2 * TILE
OPP, RIGHT, LEFT, OWN, REST = range(5)
REST_0, REST_1, MAIN_0, MAIN_1 = range(4)


def adam_step(grad, moment, second, master, refcopy):
    moment_new = beta_one * moment + (1.0 - beta_one) * grad
    second_new = beta_two * second + (1.0 - beta_two) * grad * grad
    update = moment_new / correct_one / (jnp.sqrt(second_new / correct_two) + 1e-08)
    master_new = master - learn_rate * (update + decay_rate * master)
    ref_new = blend_rate * master_new + (1.0 - blend_rate) * refcopy
    return (master_new, moment_new, second_new, ref_new, master_new.astype(BF16))


def adam_weights(grad, moment, second, master):
    return adam_step(grad, moment, second, master, master)[4]


def place():
    dp, tensor = lax.axis_index("dp"), lax.axis_index("tensor")
    x = dp // 2
    z = (tensor // 8) * 2 + dp % 2
    y = (tensor % 8) // 2
    return x, y, z, tensor % 2


def device(x, y, z, core):
    return (x * 2 + z % 2, (z // 2) * 8 + y * 2 + core)


def group_of(x, z):
    return x * 4 + (z % 2) * 2 + z // 2


def first_row(y):
    return pl.multiple_of(8 * ((5 * y) // 2), 8)


def columns(block, width):
    return pl.ds(pl.multiple_of(block * width, width), width)


def remote(src, dst, send, recv, to):
    return pltpu.make_async_remote_copy(
        src_ref=src, dst_ref=dst, send_sem=send, recv_sem=recv, device_id=to, device_id_type=MESH
    )


def loop(first, last, step):
    def run(i, carry):
        step(i)
        return carry

    lax.fori_loop(first, last, run, 0)


class Near:
    def __init__(self):
        self.x, self.y, self.z, self.core = place()
        x, y, z, core = self.x, self.y, self.z, self.core
        self.dp = x * 2 + z % 2
        self.twin = z % 2
        self.a = x * (1 - core) + z * core
        self.b = x * core + z * (1 - core)
        self.right = device(x, (y + 1) % 4, z, core)
        self.left = device(x, (y + 3) % 4, z, core)
        self.mate = device(x, y, z, 1 - core)
        self.beside = device(x, y, z + 1 - 2 * (z % 2), core)

    def along_a(self, k):
        core = self.core
        return device((self.x + k * (1 - core)) % 4, self.y, (self.z + k * core) % 4, core)

    def along_b(self, k):
        core = self.core
        return device((self.x + k * core) % 4, self.y, (self.z + k * (1 - core)) % 4, core)

    def along_x(self, k):
        return device((self.x + k) % 4, self.y, self.z, self.core)

    def line(self, i):
        py, pc = (self.y + i // 2) % 4, (self.core + i % 2) % 2
        return device(self.x, py, self.z, pc), py, pc

    def group(self, a, b):
        core = self.core
        return group_of(a * (1 - core) + b * core, a * core + b * (1 - core))

    def greet(self):
        barrier = pltpu.get_barrier_semaphore()

        def signal(to):
            pl.semaphore_signal(barrier, inc=1, device_id=to, device_id_type=MESH)

        loop(1, 4, lambda k: signal(self.along_a(k)))
        loop(1, 4, lambda k: signal(self.along_b(k)))
        loop(1, 8, lambda i: signal(self.line(i)[0]))
        pl.semaphore_wait(barrier, 13)


def step_kernel(
    text_hbm, vision_hbm, text_states, vision_states, text_sum, vision_sum, text_out, vision_out,
    mine, other, paired, over_a, over_b, from_left, from_right, total, rest, first_in, first_sum, second_in, reduced,
    rest_part, rest_line, sums, rest_sums, windows, upper, lower_own, lower_in, lower_sum, cross_out, cross_in, lower_x,
    text_state, vision_raw, vision_state, dense, staged, staged_rest, line_in, line_rest, packed,
    text_w, plane, main, rest_w, from_pair,
    load_sem, text_load, state_load, pair_s, pair_r, y_s, y_r, first_s, first_r, second_s, second_r, rest_y_s, rest_y_r,
    win_s, win_r, text_s, text_r, text2_s, text2_r,
    line_s, line_r, plane1_s, plane1_r, plane2_s, plane2_r, back_s, back_r, mate_s, mate_r, spread_s, spread_r,
    own_sem, out_sem,
):
    near = Near()
    x, y, core = near.x, near.y, near.core
    half_rows = text_hbm.shape[0] // 2
    blocks = [(y + 2) % 4, (y + 1) % 4, (y + 3) % 4, y, 4]
    order = (OPP, RIGHT, LEFT, REST, OWN)

    def loads(role):
        cols = columns(blocks[role], COLS)
        return (
            pltpu.make_async_copy(vision_hbm.at[1 - core, :, :, cols], other.at[role], load_sem.at[role, 0]),
            pltpu.make_async_copy(vision_hbm.at[core, :, :, cols], mine.at[role], load_sem.at[role, 1]),
        )

    def text_block(half, block):
        return text_hbm.at[pl.ds(half * half_rows, half_rows), columns(block, COLS)]

    def upper_load(q):
        return pltpu.make_async_copy(text_block(0, 2 * x + q), upper.at[0, q], text_load.at[q])

    def lower_load(px):
        return pltpu.make_async_copy(text_block(1, 2 * px + near.twin), lower_own.at[px], text_load.at[2 + px])

    def state_copies(i):
        return (
            pltpu.make_async_copy(text_states[i], text_state.at[i], state_load.at[i, 0]),
            pltpu.make_async_copy(vision_states[i], vision_raw.at[i], state_load.at[i, 1]),
        )

    for role in order:
        for copy in loads(role):
            copy.start()
    loop(0, 2, lambda q: upper_load(q).start())
    loop(0, 4, lambda px: lower_load(px).start())
    for i in range(3):
        for copy in state_copies(i):
            copy.start()

    near.greet()

    def upper_copy(k, q):
        to = (x + k) % 4
        return remote(
            text_block(0, 2 * to + q), upper.at[k, q], text_s.at[k, q], text_r.at[k, q], near.along_x(k)
        )

    def lower_copy(px):
        return remote(
            text_block(1, 2 * px + 1 - near.twin), lower_in.at[px], text_s.at[4 + px, 0], text_r.at[4 + px, 0],
            near.beside,
        )

    def pair(role):
        return remote(other.at[role], paired.at[role], pair_s.at[role], pair_r.at[role], near.mate)

    for role in order:
        loads(role)[0].wait()
        pair(role).start()

    for k in range(1, 4):
        for q in range(2):
            upper_copy(k, q).start()
    loop(0, 4, lambda px: lower_copy(px).start())

    def ready(role):
        loads(role)[1].wait()
        pair(role).wait_recv()

    def add_pair(role):
        ready(role)

        def add(g):
            both = mine[role, g] + paired[role, g]
            reduced[role, 0, g] = both[:, :TILE]
            reduced[role, 1, g] = both[:, TILE:]

        loop(0, GROUPS, add)

    def add_rest():
        ready(REST)

        def add(i):
            a, b = i // 4, i % 4
            g = near.group(a, b)
            both = mine[REST, g] + paired[REST, g]
            rest[0, a, b] = both[:, :TILE]
            rest[1, a, b] = both[:, TILE:]

        loop(0, GROUPS, add)

    half_a, half_b = pl.ds(0, 8), pl.ds(8, 8)

    def along(tile):
        def go(src, dst, i, to):
            return remote(src, dst, y_s.at[tile, i], y_r.at[tile, i], to)

        return [
            go(reduced.at[OPP, tile, half_a], over_a.at[tile], 0, near.right),
            go(reduced.at[OPP, tile, half_b], over_b.at[tile], 1, near.left),
            go(reduced.at[RIGHT, tile, half_b], from_left.at[tile, half_b], 2, near.right),
            go(reduced.at[LEFT, tile, half_a], from_right.at[tile, half_a], 3, near.left),
            go(reduced.at[RIGHT, tile, half_a], from_left.at[tile, half_a], 4, near.right),
            go(reduced.at[LEFT, tile, half_b], from_right.at[tile, half_b], 5, near.left),
        ]

    line = [along(0), along(1)]

    def pass_on(tile):
        line[tile][0].wait_recv()

        def add_a(g):
            reduced[RIGHT, tile, g] = reduced[RIGHT, tile, g] + over_a[tile, g]

        loop(0, 8, add_a)
        line[tile][4].start()
        line[tile][1].wait_recv()

        def add_b(g):
            reduced[LEFT, tile, 8 + g] = reduced[LEFT, tile, 8 + g] + over_b[tile, g]

        loop(0, 8, add_b)
        line[tile][5].start()

    def add_line(tile):
        for copy in line[tile][2:]:
            copy.wait_recv()

        def add(i):
            a, b = i // 4, i % 4
            g = near.group(a, b)
            total[tile, a, b] = (
                reduced[OWN, tile, g].astype(F32) + from_left[tile, g].astype(F32) + from_right[tile, g].astype(F32)
            ).astype(BF16)

        loop(0, GROUPS, add)

    def source(part):
        return rest.at[part] if part < MAIN_0 else total.at[part - MAIN_0]

    def first_copy(part, k):
        return remote(
            source(part).at[(near.a + k) % 4], first_in.at[part, k], first_s.at[part, k], first_r.at[part, k],
            near.along_a(k),
        )

    def second_copy(part, k):
        return remote(
            first_sum.at[part, (near.b + k) % 4], second_in.at[part, k], second_s.at[part, k], second_r.at[part, k],
            near.along_b(k),
        )

    def first_step(part):
        loop(1, 4, lambda k: first_copy(part, k).start())

    def second_step(part):
        loop(1, 4, lambda k: first_copy(part, k).wait_recv())
        own = source(part).at[near.a]

        def add(b):
            acc = own[b].astype(F32)
            for k in range(1, 4):
                acc = acc + first_in[part, k, b].astype(F32)
            first_sum[part, b] = acc.astype(BF16)

        loop(0, 4, add)
        loop(1, 4, lambda k: second_copy(part, k).start())

    def last_step(part):
        loop(1, 4, lambda k: second_copy(part, k).wait_recv())
        acc = first_sum[part, near.b].astype(F32)
        for k in range(1, 4):
            acc = acc + second_in[part, k].astype(F32)
        return acc

    def cross_copy():
        return remote(cross_out, cross_in, text2_s.at[0], text2_r.at[0], near.beside)

    def lower_x_copy(k):
        return remote(
            lower_sum.at[(x + k) % 4], lower_x.at[k], text2_s.at[k], text2_r.at[k], near.along_x(k)
        )

    def text_middle():
        loop(0, 2, lambda q: upper_load(q).wait())
        for k in range(1, 4):
            for q in range(2):
                upper_copy(k, q).wait_recv()

        def add_upper(i):
            rows = pl.ds(pl.multiple_of(i * 32, 32), 32)
            acc_out = upper[0, 1 - near.twin, rows].astype(F32)
            acc_own = upper[0, near.twin, rows].astype(F32)
            for k in range(1, 4):
                acc_out = acc_out + upper[k, 1 - near.twin, rows].astype(F32)
                acc_own = acc_own + upper[k, near.twin, rows].astype(F32)
            cross_out[rows] = acc_out.astype(BF16)
            text_sum[rows] = acc_own

        loop(0, half_rows // 32, add_upper)
        cross_copy().start()
        loop(0, 4, lambda px: lower_load(px).wait())
        loop(0, 4, lambda px: lower_copy(px).wait_recv())

        def add_lower(i):
            px, rows = i // 4, pl.ds(pl.multiple_of((i % 4) * 64, 64), 64)
            lower_sum[px, rows] = lower_own[px, rows] + lower_in[px, rows]

        loop(0, half_rows // 16, add_lower)
        loop(1, 4, lambda k: lower_x_copy(k).start())

    def text_weights(rows, grad):
        text_sum[rows] = grad
        text_w[rows] = adam_weights(grad, *[text_state[i, rows] for i in range(3)])

    def text_last():
        for i in range(3):
            state_copies(i)[0].wait()
        cross_copy().wait_recv()
        loop(1, 4, lambda k: lower_x_copy(k).wait_recv())

        def add(i):
            rows = pl.ds(pl.multiple_of(i * 32, 32), 32)
            text_weights(rows, text_sum[rows] + cross_in[rows].astype(F32))
            acc = lower_own[x, rows].astype(F32) + lower_in[x, rows].astype(F32)
            for k in range(1, 4):
                acc = acc + lower_x[k, rows].astype(F32)
            text_weights(pl.ds(pl.multiple_of(half_rows + i * 32, 32), 32), acc)

        loop(0, half_rows // 32, add)

    def rest_line_copy(k):
        return remote(
            rest_part, rest_line.at[k], rest_y_s.at[k], rest_y_r.at[k], device(x, (y + k) % 4, near.z, core)
        )

    own_rows = pl.ds(first_row(y), 24)

    def rest_win():
        return remote(
            rest_sums.at[:, own_rows], windows.at[core, pl.ds(8, 2)], win_s.at[0, 0], win_r.at[0, 0], near.mate
        )

    def win_copy(tile, i):
        to, py, _ = near.line(i)
        return remote(
            sums.at[tile, pl.ds(first_row(py), 24)], windows.at[core, 2 * y + tile], win_s.at[tile, i], win_r.at[tile, i],
            to,
        )

    def main_last(tile):
        sums[tile] = last_step(MAIN_0 + tile)
        loop(1, 8, lambda i: win_copy(tile, i).start())
        windows[core, 2 * y + tile] = sums[tile, own_rows]

    def rest_last():
        loop(1, 4, lambda k: rest_line_copy(k).wait_recv())
        for tile in range(2):
            acc = rest_part[tile].astype(F32)
            for k in range(1, 4):
                acc = acc + rest_line[k, tile].astype(F32)
            rest_sums[tile] = acc
            windows[core, 8 + tile] = rest_sums[tile, own_rows]
        rest_win().start()

    def arrange_states():
        for i in range(3):
            state_copies(i)[1].wait()
        for i in range(3):
            for layer in range(2):
                vision_state[i, layer] = jnp.zeros(vision_state.shape[2:], F32)
                for r in range(10):
                    vision_state[i, layer, r : r + 1, :] = vision_raw[i, r, layer : layer + 1, :]
        for layer in range(2):
            dense[layer] = jnp.zeros(dense.shape[1:], F32)

    odd = y % 2 == 1

    def weights_of(tiles):
        for layer in range(2):
            for t in tiles:
                window = windows[layer, t]
                first = jnp.where(odd, window[4:14], window[0:10])
                second = jnp.where(odd, window[14:24], window[10:20])
                dense[layer, 0:10, t * TILE : (t + 1) * TILE] = jnp.where(core == 1, second, first)

        def weights(layer, t):
            cols = slice(t * TILE, (t + 1) * TILE)
            return adam_weights(dense[layer, :, cols], *[vision_state[i, layer, :, cols] for i in range(3)])

        return weights

    def line_copy(tile, i):
        to, py, pc = near.line(i)
        return remote(
            staged.at[tile, pc, py], line_in.at[tile, y * 2 + core], line_s.at[tile, i], line_r.at[tile, i], to
        )

    def line_rest_copy(i):
        to, _, pc = near.line(i)
        return remote(staged_rest.at[pc], line_rest.at[y * 2 + core], line_s.at[2, i], line_r.at[2, i], to)

    def owner_main(tile):
        loop(1, 8, lambda i: win_copy(tile, i).wait_recv())
        weights = weights_of([2 * py + tile for py in range(4)])
        for layer in range(2):
            for py in range(4):
                staged[tile, layer, py] = weights(layer, 2 * py + tile)
        loop(1, 8, lambda i: line_copy(tile, i).start())
        line_in[tile, y * 2 + core] = staged[tile, core, y]

    def owner_rest():
        rest_win().wait_recv()
        weights = weights_of([8, 9])
        for layer in range(2):
            for tile in range(2):
                staged_rest[layer, tile] = weights(layer, 8 + tile)
        loop(1, 8, lambda i: line_rest_copy(i).start())
        line_rest[y * 2 + core] = staged_rest[core]

    def plane1(part, k):
        one = plane.at[part, near.a, near.b]
        return remote(one, one, plane1_s.at[part, k], plane1_r.at[part, k], near.along_b(k))

    def plane2(part, k):
        row = plane.at[part, near.a]
        return remote(row, row, plane2_s.at[part, k], plane2_r.at[part, k], near.along_a(k))

    def pack(part, rows_of):
        for i in range(8):
            packed[part, 10 * i : 10 * i + 10, :] = rows_of(i).astype(F32)[:10]
        plane[part, near.a, near.b] = packed[part].astype(BF16)
        loop(1, 4, lambda k: plane1(part, k).start())

    def pack_main(tile):
        loop(1, 8, lambda i: line_copy(tile, i).wait_recv())
        pack(MAIN_0 + tile, lambda i: line_in[tile, i])

    def pack_rest():
        loop(1, 8, lambda i: line_rest_copy(i).wait_recv())
        for tile in range(2):
            pack(REST_0 + tile, lambda i: line_rest[i, tile])

    def across(part):
        loop(1, 4, lambda k: plane1(part, k).wait_recv())
        loop(1, 4, lambda k: plane2(part, k).start())

    def spread(part, dst):
        loop(1, 4, lambda k: plane2(part, k).wait_recv())

        def move(i):
            a, b = i // 4, i % 4
            dst[near.group(a, b)] = plane[part, a, b]

        loop(0, GROUPS, move)

    def back(tile):
        def go(src, dst, half, i, to):
            return remote(main.at[src, tile, half], main.at[dst, tile, half], back_s.at[tile, i], back_r.at[tile, i], to)

        return [
            go(OWN, LEFT, half_a, 0, near.right),
            go(OWN, RIGHT, half_b, 1, near.left),
            go(OWN, LEFT, half_b, 2, near.right),
            go(OWN, RIGHT, half_a, 3, near.left),
            go(LEFT, OPP, half_a, 4, near.right),
            go(RIGHT, OPP, half_b, 5, near.left),
        ]

    ways = [back(0), back(1)]
    tiles = {OPP: 2 * blocks[OPP], RIGHT: 2 * blocks[RIGHT], LEFT: 2 * blocks[LEFT], OWN: 2 * y, REST: 8}

    def held(role, tile):
        return rest_w.at[tile] if role == REST else main.at[role, tile]

    def mate(role, tile):
        return remote(
            held(role, tile), from_pair.at[role, tile], mate_s.at[role, tile], mate_r.at[role, tile], near.mate
        )

    def write(role, tile, which):
        src = from_pair.at[role, tile] if which else held(role, tile)
        layer = 1 - core if which else core
        cols = columns(tiles[role] + tile, TILE)
        return pltpu.make_async_copy(src, vision_out.at[layer, :, :, cols], out_sem.at[role, tile, which])

    def give(role, tile):
        mate(role, tile).start()
        write(role, tile, 0).start()

    upper_rows, lower_rows = pl.ds(0, half_rows), pl.ds(half_rows, half_rows)
    own_cols = columns(near.dp, COLS)

    def own_text():
        return pltpu.make_async_copy(text_w, text_out.at[:, own_cols], own_sem)

    def beside_copy():
        return remote(
            text_w.at[upper_rows], text_out.at[upper_rows, own_cols], spread_s.at[0, 0], spread_r.at[0, 0], near.beside
        )

    def x_copy(k):
        return remote(
            text_w.at[lower_rows], text_out.at[lower_rows, own_cols], spread_s.at[0, k], spread_r.at[0, k],
            near.along_x(k),
        )

    def upper_on(k):
        both = text_out.at[upper_rows, columns(x, 2 * COLS)]
        return remote(both, both, spread_s.at[1, k], spread_r.at[1, k], near.along_x(k))

    def lower_on(px):
        one = text_out.at[lower_rows, columns(2 * px + near.twin, COLS)]
        return remote(one, one, spread_s.at[2, px], spread_r.at[2, px], near.beside)

    def text_spread():
        own_text().start()
        beside_copy().start()
        loop(1, 4, lambda k: x_copy(k).start())

    def text_spread_on():
        own_text().wait()
        beside_copy().wait_recv()
        loop(1, 4, lambda k: upper_on(k).start())
        loop(1, 4, lambda k: x_copy(k).wait_recv())
        loop(0, 4, lambda px: lower_on(px).start())

    add_pair(OPP)
    line[0][0].start()
    line[0][1].start()
    add_pair(RIGHT)
    line[0][2].start()
    add_pair(LEFT)
    line[0][3].start()
    add_rest()
    first_step(REST_0)
    first_step(REST_1)
    add_pair(OWN)
    pass_on(0)
    for copy in line[1][:4]:
        copy.start()
    arrange_states()
    second_step(REST_0)
    second_step(REST_1)
    add_line(0)
    first_step(MAIN_0)
    pass_on(1)
    text_middle()
    for tile in range(2):
        rest_part[tile] = last_step(REST_0 + tile).astype(BF16)
    loop(1, 4, lambda k: rest_line_copy(k).start())
    second_step(MAIN_0)
    rest_last()
    main_last(0)
    text_last()
    text_spread()
    owner_main(0)
    add_line(1)
    first_step(MAIN_1)
    owner_rest()
    pack_main(0)
    second_step(MAIN_1)
    across(MAIN_0)
    pack_rest()
    main_last(1)
    text_spread_on()
    spread(MAIN_0, main.at[OWN, 0])
    for copy in ways[0][:4]:
        copy.start()
    owner_main(1)
    across(REST_0)
    across(REST_1)
    give(OWN, 0)
    pack_main(1)
    ways[0][0].wait_recv()
    ways[0][4].start()
    ways[0][1].wait_recv()
    ways[0][5].start()
    across(MAIN_1)
    for tile in range(2):
        spread(REST_0 + tile, rest_w.at[tile])
        give(REST, tile)
    spread(MAIN_1, main.at[OWN, 1])
    for copy in ways[1][:4]:
        copy.start()
    give(OWN, 1)

    for tile in range(2):
        ways[tile][2].wait_recv()
        give(LEFT, tile)
        ways[tile][3].wait_recv()
        give(RIGHT, tile)
        if tile == 0:
            ways[1][0].wait_recv()
            ways[1][4].start()
            ways[1][1].wait_recv()
            ways[1][5].start()
        ways[tile][4].wait_recv()
        ways[tile][5].wait_recv()
        give(OPP, tile)

    for r in range(10):
        for layer in range(2):
            vision_sum[r, layer : layer + 1, :] = dense[layer, r : r + 1, :]
    for role in order:
        pair(role).wait_send()
    for copy in line[0] + line[1]:
        copy.wait_send()
    for k in range(1, 4):
        for q in range(2):
            upper_copy(k, q).wait_send()
    loop(0, 4, lambda px: lower_copy(px).wait_send())
    cross_copy().wait_send()
    loop(1, 4, lambda k: lower_x_copy(k).wait_send())
    for part in range(4):
        loop(1, 4, lambda k: first_copy(part, k).wait_send())
        loop(1, 4, lambda k: second_copy(part, k).wait_send())
        loop(1, 4, lambda k: plane1(part, k).wait_send())
        loop(1, 4, lambda k: plane2(part, k).wait_send())
    loop(1, 4, lambda k: rest_line_copy(k).wait_send())
    rest_win().wait_send()
    for tile in range(2):
        loop(1, 8, lambda i: win_copy(tile, i).wait_send())
        loop(1, 8, lambda i: line_copy(tile, i).wait_send())
    loop(1, 8, lambda i: line_rest_copy(i).wait_send())
    beside_copy().wait_send()
    loop(1, 4, lambda k: x_copy(k).wait_send())
    loop(1, 4, lambda k: upper_on(k).wait())
    loop(0, 4, lambda px: lower_on(px).wait())
    arrivals = [(OWN, 0), (REST, 0), (REST, 1), (OWN, 1), (LEFT, 0), (RIGHT, 0), (OPP, 0), (LEFT, 1), (RIGHT, 1), (OPP, 1)]
    for role, tile in arrivals:
        mate(role, tile).wait_recv()
        write(role, tile, 1).start()
    for copy in ways[0] + ways[1]:
        copy.wait_send()
    for role, tile in arrivals:
        mate(role, tile).wait_send()
        write(role, tile, 0).wait()
        write(role, tile, 1).wait()


def kernel_of(given):
    def run(text_hbm, vision_hbm, *refs):
        given(text_hbm, vision_hbm, refs[:3], refs[3:6], *refs[6:])

    return run


def step(text, vision, text_states, vision_states):
    rows = text.shape[0]
    half = rows // 2
    block = (GROUPS, ROWS, COLS)
    tile = (GROUPS, ROWS, TILE)
    square = (4, 4, ROWS, TILE)
    dma = pltpu.SemaphoreType.DMA
    vmem = pltpu.VMEM
    return pl.pallas_call(
        kernel_of(step_kernel),
        name="sum_step_gather",
        out_shape=(
            jax.ShapeDtypeStruct((rows, COLS), F32),
            jax.ShapeDtypeStruct(vision_states[0].shape, F32),
            jax.ShapeDtypeStruct((rows, 8 * COLS), BF16),
            jax.ShapeDtypeStruct((2, GROUPS, ROWS, 5 * COLS), BF16),
        ),
        in_specs=[pl.BlockSpec(memory_space=pltpu.HBM)] * 8,
        out_specs=[pl.BlockSpec(memory_space=pltpu.VMEM)] * 2 + [pl.BlockSpec(memory_space=pltpu.HBM)] * 2,
        scratch_shapes=[
            vmem((5,) + block, BF16),
            vmem((5,) + block, BF16),
            vmem((5,) + block, BF16),
            vmem((2, 8, ROWS, TILE), BF16),
            vmem((2, 8, ROWS, TILE), BF16),
            vmem((2,) + tile, BF16),
            vmem((2,) + tile, BF16),
            vmem((2,) + square, BF16),
            vmem((2,) + square, BF16),
            vmem((4,) + square, BF16),
            vmem((4, 4, ROWS, TILE), BF16),
            vmem((4, 4, ROWS, TILE), BF16),
            vmem((4, 2) + tile, BF16),
            vmem((2, ROWS, TILE), BF16),
            vmem((4, 2, ROWS, TILE), BF16),
            vmem((2, ROWS, TILE), F32),
            vmem((2, ROWS, TILE), F32),
            vmem((2, 10, 24, TILE), F32),
            vmem((4, 2, half, COLS), BF16),
            vmem((4, half, COLS), BF16),
            vmem((4, half, COLS), BF16),
            vmem((4, half, COLS), BF16),
            vmem((half, COLS), BF16),
            vmem((half, COLS), BF16),
            vmem((4, half, COLS), BF16),
            vmem((3, rows, COLS), F32),
            vmem((3,) + vision_states[0].shape, F32),
            vmem((3, 2, 16, 5 * COLS), F32),
            vmem((2, 16, 5 * COLS), F32),
            vmem((2, 2, 4, 16, TILE), BF16),
            vmem((2, 2, 16, TILE), BF16),
            vmem((2, 8, 16, TILE), BF16),
            vmem((8, 2, 16, TILE), BF16),
            vmem((4, ROWS, TILE), F32),
            vmem((rows, COLS), BF16),
            vmem((4,) + square, BF16),
            vmem((4, 2) + tile, BF16),
            vmem((2,) + tile, BF16),
            vmem((5, 2) + tile, BF16),
            dma((5, 2)),
            dma((6,)),
            dma((3, 2)),
            dma((5,)), dma((5,)),
            dma((2, 6)), dma((2, 6)),
            dma((4, 4)), dma((4, 4)),
            dma((4, 4)), dma((4, 4)),
            dma((4,)), dma((4,)),
            dma((2, 8)), dma((2, 8)),
            dma((8, 2)), dma((8, 2)),
            dma((4,)), dma((4,)),
            dma((3, 8)), dma((3, 8)),
            dma((4, 4)), dma((4, 4)),
            dma((4, 4)), dma((4, 4)),
            dma((2, 6)), dma((2, 6)),
            dma((5, 2)), dma((5, 2)),
            dma((3, 4)), dma((3, 4)),
            dma,
            dma((5, 2, 2)),
        ],
        compiler_params=pltpu.CompilerParams(collective_id=1, has_side_effects=True, vmem_limit_bytes=40 << 20),
    )(*[pltpu.with_memory_space_constraint(array, pltpu.HBM) for array in (text, vision, *text_states, *vision_states)])


def finish_kernel(*refs):
    text, vision, text_full, vision_full = refs[:5], refs[5:10], refs[10], refs[11]
    outs, vision_w = refs[12:22], refs[21]
    text_made, vision_made, sem = refs[22:]
    text_w = outs[4]
    copies = [
        pltpu.make_async_copy(vision_full, vision_w, sem.at[0]),
        pltpu.make_async_copy(text_full, text_w, sem.at[1]),
    ]
    for copy in copies:
        copy.start()

    def one(i):
        rows = pl.ds(pl.multiple_of(i * 32, 32), 32)
        made = adam_step(*[ref[rows] for ref in text])
        for j in range(4):
            text_made[j, rows] = made[j]

    loop(0, text_made.shape[1] // 32, one)
    for j in range(4):
        copies.append(pltpu.make_async_copy(text_made.at[j], outs[j], sem.at[2 + j]))
        copies[-1].start()

    def row(r):
        made = adam_step(*[ref[r] for ref in vision])
        for j in range(4):
            vision_made[j, r] = made[j]

    loop(0, vision_made.shape[1], row)
    for j in range(4):
        copies.append(pltpu.make_async_copy(vision_made.at[j], outs[5 + j], sem.at[6 + j]))
        copies[-1].start()
    for copy in copies:
        copy.wait()


def finish(text, vision, text_full, vision_full):
    def like(array):
        return jax.ShapeDtypeStruct(array.shape, array.dtype)

    in_hbm, in_vmem = pl.BlockSpec(memory_space=pltpu.HBM), pl.BlockSpec(memory_space=pltpu.VMEM)
    return pl.pallas_call(
        finish_kernel,
        name="write_results",
        out_shape=(like(text[0]),) * 4 + (like(text_full),) + (like(vision[0]),) * 4 + (like(vision_full),),
        in_specs=[in_vmem] * 10 + [in_hbm] * 2,
        out_specs=[in_hbm] * 10,
        scratch_shapes=[
            pltpu.VMEM((4,) + text[0].shape, F32),
            pltpu.VMEM((4,) + vision[0].shape, F32),
            pltpu.SemaphoreType.DMA((10,)),
        ],
        compiler_params=pltpu.CompilerParams(vmem_limit_bytes=16 << 20),
    )(*text, *vision, text_full, vision_full)


def body(
    text_grads, text_master, text_moment, text_second, text_ref,
    vision_grads, vision_master, vision_moment, vision_second, vision_ref,
):
    layers, width = vision_grads.shape[1], vision_grads.shape[3]
    text_states = (text_moment, text_second, text_master, text_ref)
    vision_states = tuple(
        jnp.transpose(array, (1, 0, 2)) for array in (vision_moment, vision_second, vision_master, vision_ref)
    )
    text_total, vision_total, text_full, vision_full = step(
        text_grads[0], vision_grads.reshape(layers, GROUPS, ROWS, width), text_states[:3], vision_states[:3]
    )
    outs = finish((text_total,) + text_states, (vision_total,) + vision_states, text_full, vision_full)
    vision_out = tuple(jnp.transpose(array, (1, 0, 2)) for array in outs[5:9])
    return outs[:5] + vision_out + (outs[9].reshape(layers, width, width),)


def solution(mesh):
    owned = P("tensor", "dp")
    vision_owned = P(None, ("dp", "tensor"), None)
    return jax.shard_map(
        body,
        mesh=mesh,
        in_specs=(P("dp", "tensor", None),) + (owned,) * 4 + (P(("dp", "tensor"), None, None, None),) + (vision_owned,) * 4,
        out_specs=(owned,) * 4 + (P("tensor", None),) + (vision_owned,) * 4 + (P(),),
        check_vma=False,
    )
```

```python
import functools

import jax
import jax.numpy as jnp
from jax import lax
from jax.experimental import pallas as pl
from jax.experimental.pallas import tpu as pltpu
from jax.sharding import PartitionSpec as P

MESH = pl.DeviceIdType.MESH
BF16, F32 = jnp.bfloat16, jnp.float32

beta_one = 0.9
beta_two = 0.95
correct_one = 1.0 - 0.9**10
correct_two = 1.0 - 0.95**10
learn_rate = 0.01
decay_rate = 0.1
blend_rate = 0.6

GROUPS = 16
ROWS = 80
TILE = 128
COLS = 2 * TILE
OPP, RIGHT, LEFT, OWN, REST = range(5)
REST_0, REST_1, MAIN_0, MAIN_1 = range(4)


def adam_step(grad, moment, second, master, refcopy):
    moment_new = beta_one * moment + (1.0 - beta_one) * grad
    second_new = beta_two * second + (1.0 - beta_two) * grad * grad
    update = moment_new / correct_one / (jnp.sqrt(second_new / correct_two) + 1e-08)
    master_new = master - learn_rate * (update + decay_rate * master)
    ref_new = blend_rate * master_new + (1.0 - blend_rate) * refcopy
    return (master_new, moment_new, second_new, ref_new, master_new.astype(BF16))


def adam_weights(grad, moment, second, master):
    return adam_step(grad, moment, second, master, master)[4]


def place():
    dp, tensor = lax.axis_index("dp"), lax.axis_index("tensor")
    x = dp // 2
    z = (tensor // 8) * 2 + dp % 2
    y = (tensor % 8) // 2
    return x, y, z, tensor % 2


def device(x, y, z, core):
    return (x * 2 + z % 2, (z // 2) * 8 + y * 2 + core)


def group_of(x, z):
    return x * 4 + (z % 2) * 2 + z // 2


def first_row(y):
    return pl.multiple_of(8 * ((5 * y) // 2), 8)


def columns(block, width):
    return pl.ds(pl.multiple_of(block * width, width), width)


def remote(src, dst, send, recv, to):
    return pltpu.make_async_remote_copy(
        src_ref=src, dst_ref=dst, send_sem=send, recv_sem=recv, device_id=to, device_id_type=MESH
    )


def loop(first, last, step):
    def run(i, carry):
        step(i)
        return carry

    lax.fori_loop(first, last, run, 0)


class Near:
    def __init__(self):
        self.x, self.y, self.z, self.core = place()
        x, y, z, core = self.x, self.y, self.z, self.core
        self.dp = x * 2 + z % 2
        self.twin = z % 2
        self.a = x * (1 - core) + z * core
        self.b = x * core + z * (1 - core)
        self.right = device(x, (y + 1) % 4, z, core)
        self.left = device(x, (y + 3) % 4, z, core)
        self.mate = device(x, y, z, 1 - core)
        self.beside = device(x, y, z + 1 - 2 * (z % 2), core)

    def along_a(self, k):
        core = self.core
        return device((self.x + k * (1 - core)) % 4, self.y, (self.z + k * core) % 4, core)

    def along_b(self, k):
        core = self.core
        return device((self.x + k * core) % 4, self.y, (self.z + k * (1 - core)) % 4, core)

    def along_x(self, k):
        return device((self.x + k) % 4, self.y, self.z, self.core)

    def line(self, i):
        py, pc = (self.y + i // 2) % 4, (self.core + i % 2) % 2
        return device(self.x, py, self.z, pc), py, pc

    def group(self, a, b):
        core = self.core
        return group_of(a * (1 - core) + b * core, a * core + b * (1 - core))

    def greet(self):
        barrier = pltpu.get_barrier_semaphore()

        def signal(to):
            pl.semaphore_signal(barrier, inc=1, device_id=to, device_id_type=MESH)

        loop(1, 4, lambda k: signal(self.along_a(k)))
        loop(1, 4, lambda k: signal(self.along_b(k)))
        loop(1, 8, lambda i: signal(self.line(i)[0]))
        pl.semaphore_wait(barrier, 13)


def step_kernel(
    text_hbm, vision_hbm, text_states, vision_states, text_sum, vision_sum, text_out, vision_out,
    mine, other, paired, over_a, over_b, from_left, from_right, total, rest, first_in, first_sum, second_in, reduced,
    sums, rest_sums, windows, rest_windows, upper, lower_own, lower_in, lower_sum, cross_out, cross_in, lower_x,
    text_state, vision_raw, own_state, line_state, tile_state, dense, staged_rest, line_rest, packed, text_w, plane,
    load_sem, text_load, state_load, pair_s, pair_r, y_s, y_r, first_s, first_r, second_s, second_r,
    state_s, state_r, win_s, win_r, rest_win_s, rest_win_r, text_s, text_r, text2_s, text2_r,
    line_s, line_r, plane1_s, plane1_r, plane2_s, plane2_r, back_s, back_r, mate_s, mate_r, spread_s, spread_r,
    own_sem,
):
    near = Near()
    x, y, core = near.x, near.y, near.core
    half_rows = text_hbm.shape[0] // 2
    blocks = [(y + 2) % 4, (y + 1) % 4, (y + 3) % 4, y, 4]
    order = (OPP, RIGHT, LEFT, REST, OWN)

    def loads(role):
        cols = columns(blocks[role], COLS)
        return (
            pltpu.make_async_copy(vision_hbm.at[1 - core, :, :, cols], other.at[role], load_sem.at[role, 0]),
            pltpu.make_async_copy(vision_hbm.at[core, :, :, cols], mine.at[role], load_sem.at[role, 1]),
        )

    def text_block(half, block):
        return text_hbm.at[pl.ds(half * half_rows, half_rows), columns(block, COLS)]

    def upper_load(q):
        return pltpu.make_async_copy(text_block(0, 2 * x + q), upper.at[0, q], text_load.at[q])

    def lower_load(px):
        return pltpu.make_async_copy(text_block(1, 2 * px + near.twin), lower_own.at[px], text_load.at[2 + px])

    def state_copies(i):
        return (
            pltpu.make_async_copy(text_states[i], text_state.at[i], state_load.at[i, 0]),
            pltpu.make_async_copy(vision_states[i], vision_raw.at[i], state_load.at[i, 1]),
        )

    for copy in loads(OPP):
        copy.start()
    for i in range(3):
        state_copies(i)[1].start()
    for role in order[1:]:
        for copy in loads(role):
            copy.start()
    loop(0, 2, lambda q: upper_load(q).start())
    loop(0, 4, lambda px: lower_load(px).start())
    for i in range(3):
        state_copies(i)[0].start()

    near.greet()

    def upper_copy(k, q):
        to = (x + k) % 4
        return remote(
            text_block(0, 2 * to + q), upper.at[k, q], text_s.at[k, q], text_r.at[k, q], near.along_x(k)
        )

    def lower_copy(px):
        return remote(
            text_block(1, 2 * px + 1 - near.twin), lower_in.at[px], text_s.at[4 + px, 0], text_r.at[4 + px, 0],
            near.beside,
        )

    def pair(role):
        return remote(other.at[role], paired.at[role], pair_s.at[role], pair_r.at[role], near.mate)

    def ready(role):
        loads(role)[1].wait()
        pair(role).wait_recv()

    def add_pair(role):
        ready(role)

        def add(g):
            both = mine[role, g] + paired[role, g]
            reduced[role, 0, g] = both[:, :TILE]
            reduced[role, 1, g] = both[:, TILE:]

        loop(0, GROUPS, add)

    def add_rest():
        ready(REST)

        def add(i):
            a, b = i // 4, i % 4
            g = near.group(a, b)
            both = mine[REST, g] + paired[REST, g]
            rest[0, a, b] = both[:, :TILE]
            rest[1, a, b] = both[:, TILE:]

        loop(0, GROUPS, add)

    half_a, half_b = pl.ds(0, 8), pl.ds(8, 8)

    def along(tile):
        def go(src, dst, i, to):
            return remote(src, dst, y_s.at[tile, i], y_r.at[tile, i], to)

        return [
            go(reduced.at[OPP, tile, half_a], over_a.at[tile], 0, near.right),
            go(reduced.at[OPP, tile, half_b], over_b.at[tile], 1, near.left),
            go(reduced.at[RIGHT, tile, half_b], from_left.at[tile, half_b], 2, near.right),
            go(reduced.at[LEFT, tile, half_a], from_right.at[tile, half_a], 3, near.left),
            go(reduced.at[RIGHT, tile, half_a], from_left.at[tile, half_a], 4, near.right),
            go(reduced.at[LEFT, tile, half_b], from_right.at[tile, half_b], 5, near.left),
        ]

    line = [along(0), along(1)]

    def pass_on(tile):
        line[tile][0].wait_recv()

        def add_a(g):
            reduced[RIGHT, tile, g] = reduced[RIGHT, tile, g] + over_a[tile, g]

        loop(0, 8, add_a)
        line[tile][4].start()
        line[tile][1].wait_recv()

        def add_b(g):
            reduced[LEFT, tile, 8 + g] = reduced[LEFT, tile, 8 + g] + over_b[tile, g]

        loop(0, 8, add_b)
        line[tile][5].start()

    def add_line(tile):
        for copy in line[tile][2:]:
            copy.wait_recv()

        def add(i):
            a, b = i // 4, i % 4
            g = near.group(a, b)
            total[tile, a, b] = (
                reduced[OWN, tile, g].astype(F32) + from_left[tile, g].astype(F32) + from_right[tile, g].astype(F32)
            ).astype(BF16)

        loop(0, GROUPS, add)

    def source(part):
        return rest.at[part] if part < MAIN_0 else total.at[part - MAIN_0]

    def first_copy(part, k):
        return remote(
            source(part).at[(near.a + k) % 4], first_in.at[part, k], first_s.at[part, k], first_r.at[part, k],
            near.along_a(k),
        )

    def second_copy(part, k):
        return remote(
            first_sum.at[part, (near.b + k) % 4], second_in.at[part, k], second_s.at[part, k], second_r.at[part, k],
            near.along_b(k),
        )

    def first_step(part):
        loop(1, 4, lambda k: first_copy(part, k).start())

    def second_step(part):
        loop(1, 4, lambda k: first_copy(part, k).wait_recv())
        own = source(part).at[near.a]

        def add(b):
            acc = own[b].astype(F32)
            for k in range(1, 4):
                acc = acc + first_in[part, k, b].astype(F32)
            first_sum[part, b] = acc.astype(BF16)

        loop(0, 4, add)
        loop(1, 4, lambda k: second_copy(part, k).start())

    def last_step(part):
        loop(1, 4, lambda k: second_copy(part, k).wait_recv())
        acc = first_sum[part, near.b].astype(F32)
        for k in range(1, 4):
            acc = acc + second_in[part, k].astype(F32)
        return acc

    def cross_copy():
        return remote(cross_out, cross_in, text2_s.at[0], text2_r.at[0], near.beside)

    def lower_x_copy(k):
        return remote(
            lower_sum.at[(x + k) % 4], lower_x.at[k], text2_s.at[k], text2_r.at[k], near.along_x(k)
        )

    def text_middle():
        loop(0, 2, lambda q: upper_load(q).wait())
        for k in range(1, 4):
            for q in range(2):
                upper_copy(k, q).wait_recv()

        def add_upper(i):
            rows = pl.ds(pl.multiple_of(i * 32, 32), 32)
            acc_out = upper[0, 1 - near.twin, rows].astype(F32)
            acc_own = upper[0, near.twin, rows].astype(F32)
            for k in range(1, 4):
                acc_out = acc_out + upper[k, 1 - near.twin, rows].astype(F32)
                acc_own = acc_own + upper[k, near.twin, rows].astype(F32)
            cross_out[rows] = acc_out.astype(BF16)
            text_sum[rows] = acc_own

        loop(0, half_rows // 32, add_upper)
        cross_copy().start()
        loop(0, 4, lambda px: lower_load(px).wait())
        loop(0, 4, lambda px: lower_copy(px).wait_recv())

        def add_lower(i):
            px, rows = i // 4, pl.ds(pl.multiple_of((i % 4) * 64, 64), 64)
            lower_sum[px, rows] = lower_own[px, rows] + lower_in[px, rows]

        loop(0, half_rows // 16, add_lower)
        loop(1, 4, lambda k: lower_x_copy(k).start())

    def text_weights(rows, grad):
        text_sum[rows] = grad
        text_w[rows] = adam_weights(grad, *[text_state[i, rows] for i in range(3)])

    def text_last():
        for i in range(3):
            state_copies(i)[0].wait()
        cross_copy().wait_recv()
        loop(1, 4, lambda k: lower_x_copy(k).wait_recv())

        def add(i):
            rows = pl.ds(pl.multiple_of(i * 32, 32), 32)
            text_weights(rows, text_sum[rows] + cross_in[rows].astype(F32))
            acc = lower_own[x, rows].astype(F32) + lower_in[x, rows].astype(F32)
            for k in range(1, 4):
                acc = acc + lower_x[k, rows].astype(F32)
            text_weights(pl.ds(pl.multiple_of(half_rows + i * 32, 32), 32), acc)

        loop(0, half_rows // 32, add)

    def arrange_states():
        for i in range(3):
            state_copies(i)[1].wait()
        for layer in range(2):
            for i in range(3):
                for r in range(10):
                    own_state[layer, 10 * i + r : 10 * i + r + 1, :] = vision_raw[i, r, layer : layer + 1, :]

    def state_copy(i):
        to, py, pc = near.line(i)
        return remote(
            own_state.at[pc, :, columns(py, COLS)], line_state.at[y * 2 + core], state_s.at[i], state_r.at[i], to
        )

    def send_states():
        loop(1, 8, lambda i: state_copy(i).start())
        line_state[y * 2 + core] = own_state[core, :, columns(y, COLS)]

    def join_states():
        loop(1, 8, lambda i: state_copy(i).wait_recv())
        for place_on_line in range(8):
            for i in range(3):
                tile_state[i, 10 * place_on_line : 10 * place_on_line + 10, :] = line_state[
                    place_on_line, 10 * i : 10 * i + 10, :
                ]

    own_rows = pl.ds(first_row(y), 24)

    def win_copy(tile, i):
        to, py, _ = near.line(i)
        return remote(
            sums.at[tile, pl.ds(first_row(py), 24)], windows.at[core, 2 * y + tile], win_s.at[tile, i], win_r.at[tile, i],
            to,
        )

    def rest_win_copy(i):
        to, py, _ = near.line(i)
        return remote(
            rest_sums.at[:, pl.ds(first_row(py), 24)], rest_windows.at[core, y], rest_win_s.at[i], rest_win_r.at[i], to
        )

    def main_last(tile):
        part = MAIN_0 + tile
        grad = last_step(part)
        sums[tile] = grad
        cols = slice(tile * TILE, (tile + 1) * TILE)
        plane[part, near.a, near.b] = adam_weights(grad, *[tile_state[i, :, cols] for i in range(3)])
        loop(1, 4, lambda k: plane1(part, k).start())
        loop(1, 8, lambda i: win_copy(tile, i).start())
        windows[core, 2 * y + tile] = sums[tile, own_rows]

    def rest_last():
        for tile in range(2):
            rest_sums[tile] = last_step(REST_0 + tile)
        loop(1, 8, lambda i: rest_win_copy(i).start())
        rest_windows[core, y] = rest_sums[:, own_rows]

    odd = y % 2 == 1

    def own_part(window):
        first = jnp.where(odd, window[4:14], window[0:10])
        second = jnp.where(odd, window[14:24], window[10:20])
        return jnp.where(core == 1, second, first)

    def line_rest_copy(i):
        to, _, pc = near.line(i)
        return remote(staged_rest.at[pc], line_rest.at[y * 2 + core], line_s.at[i], line_r.at[i], to)

    def owner_rest():
        loop(1, 8, lambda i: rest_win_copy(i).wait_recv())
        for layer in range(2):
            for tile in range(2):
                cols = slice((8 + tile) * TILE, (9 + tile) * TILE)
                window = rest_windows[layer, 0, tile]
                for py in range(1, 4):
                    window = window + rest_windows[layer, py, tile]
                grad = own_part(window)
                dense[layer, 0:10, cols] = grad
                staged_rest[layer, tile, 0:10] = adam_weights(
                    grad, *[own_state[layer, 10 * i : 10 * i + 10, cols] for i in range(3)]
                )
        loop(1, 8, lambda i: line_rest_copy(i).start())
        line_rest[y * 2 + core] = staged_rest[core]

    def owner_main(tile):
        loop(1, 8, lambda i: win_copy(tile, i).wait_recv())
        for layer in range(2):
            for py in range(4):
                t = 2 * py + tile
                dense[layer, 0:10, t * TILE : (t + 1) * TILE] = own_part(windows[layer, t])

    def plane1(part, k):
        one = plane.at[part, near.a, near.b]
        return remote(one, one, plane1_s.at[part, k], plane1_r.at[part, k], near.along_b(k))

    def plane2(part, k):
        row = plane.at[part, near.a]
        return remote(row, row, plane2_s.at[part, k], plane2_r.at[part, k], near.along_a(k))

    def pack_rest():
        loop(1, 8, lambda i: line_rest_copy(i).wait_recv())
        for tile in range(2):
            part = REST_0 + tile
            for i in range(8):
                packed[tile, 10 * i : 10 * i + 10, :] = line_rest[i, tile].astype(F32)[:10]
            plane[part, near.a, near.b] = packed[tile].astype(BF16)
            loop(1, 4, lambda k: plane1(part, k).start())

    def across(part):
        loop(1, 4, lambda k: plane1(part, k).wait_recv())
        loop(1, 4, lambda k: plane2(part, k).start())

    first_tile = {OPP: 2 * blocks[OPP], RIGHT: 2 * blocks[RIGHT], LEFT: 2 * blocks[LEFT], OWN: 2 * y, REST: 8}

    def held(role, tile):
        return vision_out.at[core, first_tile[role] + tile]

    def spread(part, role, tile):
        loop(1, 4, lambda k: plane2(part, k).wait_recv())

        def move(i):
            a, b = i // 4, i % 4
            vision_out[core, first_tile[role] + tile, near.group(a, b)] = plane[part, a, b]

        loop(0, GROUPS, move)

    def back(tile):
        def go(role, half, i, to):
            part = held(role, tile).at[half]
            return remote(part, part, back_s.at[tile, i], back_r.at[tile, i], to)

        return [
            go(OWN, half_a, 0, near.right),
            go(OWN, half_b, 1, near.left),
            go(OWN, half_b, 2, near.right),
            go(OWN, half_a, 3, near.left),
            go(LEFT, half_a, 4, near.right),
            go(RIGHT, half_b, 5, near.left),
        ]

    ways = [back(0), back(1)]

    def mate(role, tile):
        return remote(held(role, tile), held(role, tile), mate_s.at[role, tile], mate_r.at[role, tile], near.mate)

    def give(role, tile):
        mate(role, tile).start()

    upper_rows, lower_rows = pl.ds(0, half_rows), pl.ds(half_rows, half_rows)
    own_cols = columns(near.dp, COLS)

    def own_text():
        return pltpu.make_async_copy(text_w, text_out.at[:, own_cols], own_sem)

    def beside_copy():
        return remote(
            text_w.at[upper_rows], text_out.at[upper_rows, own_cols], spread_s.at[0, 0], spread_r.at[0, 0], near.beside
        )

    def x_copy(k):
        return remote(
            text_w.at[lower_rows], text_out.at[lower_rows, own_cols], spread_s.at[0, k], spread_r.at[0, k],
            near.along_x(k),
        )

    def upper_on(k):
        both = text_out.at[upper_rows, columns(x, 2 * COLS)]
        return remote(both, both, spread_s.at[1, k], spread_r.at[1, k], near.along_x(k))

    def lower_on(px):
        one = text_out.at[lower_rows, columns(2 * px + near.twin, COLS)]
        return remote(one, one, spread_s.at[2, px], spread_r.at[2, px], near.beside)

    def text_spread():
        own_text().start()
        beside_copy().start()
        loop(1, 4, lambda k: x_copy(k).start())

    def text_spread_on():
        own_text().wait()
        beside_copy().wait_recv()
        loop(1, 4, lambda k: upper_on(k).start())
        loop(1, 4, lambda k: x_copy(k).wait_recv())
        loop(0, 4, lambda px: lower_on(px).start())

    def start_pair(role):
        loads(role)[0].wait()
        pair(role).start()

    for k in range(1, 4):
        for q in range(2):
            upper_copy(k, q).start()
    loop(0, 4, lambda px: lower_copy(px).start())
    for role in order:
        start_pair(role)
    add_pair(OPP)
    line[0][0].start()
    line[0][1].start()
    add_pair(RIGHT)
    line[0][2].start()
    add_pair(LEFT)
    line[0][3].start()
    add_rest()
    first_step(REST_0)
    first_step(REST_1)
    add_pair(OWN)
    pass_on(0)
    for copy in line[1][:4]:
        copy.start()
    arrange_states()
    send_states()
    add_line(0)
    first_step(MAIN_0)
    second_step(REST_0)
    second_step(REST_1)
    pass_on(1)
    second_step(MAIN_0)
    text_middle()
    rest_last()
    join_states()
    main_last(0)
    add_line(1)
    first_step(MAIN_1)
    across(MAIN_0)
    owner_rest()
    text_last()
    text_spread()
    second_step(MAIN_1)
    spread(MAIN_0, OWN, 0)
    for copy in ways[0][:4]:
        copy.start()
    give(OWN, 0)
    main_last(1)
    pack_rest()
    ways[0][0].wait_recv()
    ways[0][4].start()
    ways[0][1].wait_recv()
    ways[0][5].start()
    across(MAIN_1)
    across(REST_0)
    across(REST_1)
    text_spread_on()
    spread(MAIN_1, OWN, 1)
    for copy in ways[1][:4]:
        copy.start()
    give(OWN, 1)
    ways[0][2].wait_recv()
    give(LEFT, 0)
    ways[0][3].wait_recv()
    give(RIGHT, 0)
    for tile in range(2):
        spread(REST_0 + tile, REST, tile)
        give(REST, tile)
    ways[0][4].wait_recv()
    ways[0][5].wait_recv()
    give(OPP, 0)
    ways[1][0].wait_recv()
    ways[1][4].start()
    ways[1][1].wait_recv()
    ways[1][5].start()
    owner_main(0)
    owner_main(1)
    for r in range(10):
        for layer in range(2):
            vision_sum[r, layer : layer + 1, :] = dense[layer, r : r + 1, :]

    for role in order:
        pair(role).wait_send()
    for copy in line[0] + line[1]:
        copy.wait_send()
    for k in range(1, 4):
        for q in range(2):
            upper_copy(k, q).wait_send()
    loop(0, 4, lambda px: lower_copy(px).wait_send())
    cross_copy().wait_send()
    loop(1, 4, lambda k: lower_x_copy(k).wait_send())
    for part in range(4):
        loop(1, 4, lambda k: first_copy(part, k).wait_send())
        loop(1, 4, lambda k: second_copy(part, k).wait_send())
        loop(1, 4, lambda k: plane1(part, k).wait_send())
        loop(1, 4, lambda k: plane2(part, k).wait_send())
    loop(1, 8, lambda i: state_copy(i).wait_send())
    loop(1, 8, lambda i: rest_win_copy(i).wait_send())
    for tile in range(2):
        loop(1, 8, lambda i: win_copy(tile, i).wait_send())
    loop(1, 8, lambda i: line_rest_copy(i).wait_send())
    beside_copy().wait_send()
    loop(1, 4, lambda k: x_copy(k).wait_send())

    ways[1][2].wait_recv()
    give(LEFT, 1)
    ways[1][3].wait_recv()
    give(RIGHT, 1)
    ways[1][4].wait_recv()
    ways[1][5].wait_recv()
    give(OPP, 1)
    loop(1, 4, lambda k: upper_on(k).wait())
    loop(0, 4, lambda px: lower_on(px).wait())
    for copy in ways[0] + ways[1]:
        copy.wait_send()
    for role in range(5):
        for tile in range(2):
            mate(role, tile).wait()


def kernel_of(given):
    def run(text_hbm, vision_hbm, *refs):
        given(text_hbm, vision_hbm, refs[:3], refs[3:6], *refs[6:])

    return run


def step(text, vision, text_states, vision_states):
    rows = text.shape[0]
    half = rows // 2
    block = (GROUPS, ROWS, COLS)
    tile = (GROUPS, ROWS, TILE)
    square = (4, 4, ROWS, TILE)
    dma = pltpu.SemaphoreType.DMA
    vmem = pltpu.VMEM
    return pl.pallas_call(
        kernel_of(step_kernel),
        name="sum_step_gather",
        out_shape=(
            jax.ShapeDtypeStruct((rows, COLS), F32),
            jax.ShapeDtypeStruct(vision_states[0].shape, F32),
            jax.ShapeDtypeStruct((rows, 8 * COLS), BF16),
            jax.ShapeDtypeStruct((2, 10) + tile, BF16),
        ),
        in_specs=[pl.BlockSpec(memory_space=pltpu.HBM)] * 8,
        out_specs=[pl.BlockSpec(memory_space=pltpu.VMEM)] * 4,
        scratch_shapes=[
            vmem((5,) + block, BF16),
            vmem((5,) + block, BF16),
            vmem((5,) + block, BF16),
            vmem((2, 8, ROWS, TILE), BF16),
            vmem((2, 8, ROWS, TILE), BF16),
            vmem((2,) + tile, BF16),
            vmem((2,) + tile, BF16),
            vmem((2,) + square, BF16),
            vmem((2,) + square, BF16),
            vmem((4,) + square, BF16),
            vmem((4, 4, ROWS, TILE), BF16),
            vmem((4, 4, ROWS, TILE), BF16),
            vmem((4, 2) + tile, BF16),
            vmem((2, ROWS, TILE), F32),
            vmem((2, ROWS, TILE), F32),
            vmem((2, 8, 24, TILE), F32),
            vmem((2, 4, 2, 24, TILE), F32),
            vmem((4, 2, half, COLS), BF16),
            vmem((4, half, COLS), BF16),
            vmem((4, half, COLS), BF16),
            vmem((4, half, COLS), BF16),
            vmem((half, COLS), BF16),
            vmem((half, COLS), BF16),
            vmem((4, half, COLS), BF16),
            vmem((3, rows, COLS), F32),
            vmem((3,) + vision_states[0].shape, F32),
            vmem((2, 32, 5 * COLS), F32),
            vmem((8, 32, COLS), F32),
            vmem((3, ROWS, COLS), F32),
            vmem((2, 16, 5 * COLS), F32),
            vmem((2, 2, 16, TILE), BF16),
            vmem((8, 2, 16, TILE), BF16),
            vmem((2, ROWS, TILE), F32),
            vmem((rows, COLS), BF16),
            vmem((4,) + square, BF16),
            dma((5, 2)),
            dma((6,)),
            dma((3, 2)),
            dma((5,)), dma((5,)),
            dma((2, 6)), dma((2, 6)),
            dma((4, 4)), dma((4, 4)),
            dma((4, 4)), dma((4, 4)),
            dma((8,)), dma((8,)),
            dma((2, 8)), dma((2, 8)),
            dma((8,)), dma((8,)),
            dma((8, 2)), dma((8, 2)),
            dma((4,)), dma((4,)),
            dma((8,)), dma((8,)),
            dma((4, 4)), dma((4, 4)),
            dma((4, 4)), dma((4, 4)),
            dma((2, 6)), dma((2, 6)),
            dma((5, 2)), dma((5, 2)),
            dma((3, 4)), dma((3, 4)),
            dma,
        ],
        compiler_params=pltpu.CompilerParams(collective_id=1, has_side_effects=True, vmem_limit_bytes=40 << 20),
    )(*[pltpu.with_memory_space_constraint(array, pltpu.HBM) for array in (text, vision, *text_states, *vision_states)])


def finish_kernel(*refs):
    text, vision, text_full, vision_full = refs[:5], refs[5:10], refs[10], refs[11]
    outs, vision_w = refs[12:22], refs[21]
    text_made, vision_made, sem, tile_sem = refs[22:]
    text_w = outs[4]
    copies = [
        pltpu.make_async_copy(vision_full.at[layer, t], vision_w.at[layer, :, :, t * TILE : (t + 1) * TILE], tile_sem.at[layer, t])
        for layer in range(2)
        for t in range(10)
    ]
    copies.append(pltpu.make_async_copy(text_full, text_w, sem.at[1]))
    for copy in copies:
        copy.start()

    def one(i):
        rows = pl.ds(pl.multiple_of(i * 32, 32), 32)
        made = adam_step(*[ref[rows] for ref in text])
        for j in range(4):
            text_made[j, rows] = made[j]

    loop(0, text_made.shape[1] // 32, one)
    for j in range(4):
        copies.append(pltpu.make_async_copy(text_made.at[j], outs[j], sem.at[2 + j]))
        copies[-1].start()

    def row(r):
        made = adam_step(*[ref[r] for ref in vision])
        for j in range(4):
            vision_made[j, r] = made[j]

    loop(0, vision_made.shape[1], row)
    for j in range(4):
        copies.append(pltpu.make_async_copy(vision_made.at[j], outs[5 + j], sem.at[6 + j]))
        copies[-1].start()
    for copy in copies:
        copy.wait()


def finish(text, vision, text_full, vision_full):
    def like(array):
        return jax.ShapeDtypeStruct(array.shape, array.dtype)

    in_hbm, in_vmem = pl.BlockSpec(memory_space=pltpu.HBM), pl.BlockSpec(memory_space=pltpu.VMEM)
    return pl.pallas_call(
        finish_kernel,
        name="write_results",
        out_shape=(like(text[0]),) * 4
        + (like(text_full),)
        + (like(vision[0]),) * 4
        + (jax.ShapeDtypeStruct((2, GROUPS, ROWS, 5 * COLS), BF16),),
        in_specs=[in_vmem] * 10 + [in_hbm] * 2,
        out_specs=[in_hbm] * 10,
        scratch_shapes=[
            pltpu.VMEM((4,) + text[0].shape, F32),
            pltpu.VMEM((4,) + vision[0].shape, F32),
            pltpu.SemaphoreType.DMA((10,)),
            pltpu.SemaphoreType.DMA((2, 10)),
        ],
        compiler_params=pltpu.CompilerParams(vmem_limit_bytes=16 << 20),
    )(*text, *vision, text_full, vision_full)


def body(
    text_grads, text_master, text_moment, text_second, text_ref,
    vision_grads, vision_master, vision_moment, vision_second, vision_ref,
):
    layers, width = vision_grads.shape[1], vision_grads.shape[3]
    text_states = (text_moment, text_second, text_master, text_ref)
    vision_states = tuple(
        jnp.transpose(array, (1, 0, 2)) for array in (vision_moment, vision_second, vision_master, vision_ref)
    )
    text_total, vision_total, text_full, vision_full = step(
        text_grads[0], vision_grads.reshape(layers, GROUPS, ROWS, width), text_states[:3], vision_states[:3]
    )
    outs = finish((text_total,) + text_states, (vision_total,) + vision_states, text_full, vision_full)
    vision_out = tuple(jnp.transpose(array, (1, 0, 2)) for array in outs[5:9])
    return outs[:5] + vision_out + (outs[9].reshape(layers, width, width),)


def solution(mesh):
    owned = P("tensor", "dp")
    vision_owned = P(None, ("dp", "tensor"), None)
    return jax.shard_map(
        body,
        mesh=mesh,
        in_specs=(P("dp", "tensor", None),) + (owned,) * 4 + (P(("dp", "tensor"), None, None, None),) + (vision_owned,) * 4,
        out_specs=(owned,) * 4 + (P("tensor", None),) + (vision_owned,) * 4 + (P(),),
        check_vma=False,
    )
```

```python
import functools

import jax
import jax.numpy as jnp
from jax import lax
from jax.experimental import pallas as pl
from jax.experimental.pallas import tpu as pltpu
from jax.sharding import PartitionSpec as P

MESH = pl.DeviceIdType.MESH
BF16, F32 = jnp.bfloat16, jnp.float32

beta_one = 0.9
beta_two = 0.95
correct_one = 1.0 - 0.9**10
correct_two = 1.0 - 0.95**10
learn_rate = 0.01
decay_rate = 0.1
blend_rate = 0.6

GROUPS = 16
ROWS = 80
TILE = 128
UPPER = 9
COLS = 2 * TILE
OPP, RIGHT, LEFT, OWN, REST = range(5)
PIECES = ((0, 0, 32), (0, 32, 48), (1, 0, 48), (1, 48, 32))
UNITS = ((0, 0, 2 * ROWS),) + tuple((1 + tile, first, n) for tile, first, n in PIECES)


def adam_step(grad, moment, second, master, refcopy):
    moment_new = beta_one * moment + (1.0 - beta_one) * grad
    second_new = beta_two * second + (1.0 - beta_two) * grad * grad
    update = moment_new / correct_one / (jnp.sqrt(second_new / correct_two) + 1e-08)
    master_new = master - learn_rate * (update + decay_rate * master)
    ref_new = blend_rate * master_new + (1.0 - blend_rate) * refcopy
    return (master_new, moment_new, second_new, ref_new, master_new.astype(BF16))


def adam_weights(grad, moment, second, master):
    return adam_step(grad, moment, second, master, master)[4]


def place():
    dp, tensor = lax.axis_index("dp"), lax.axis_index("tensor")
    x = dp // 2
    z = (tensor // 8) * 2 + dp % 2
    y = (tensor % 8) // 2
    return x, y, z, tensor % 2


def device(x, y, z, core):
    return (x * 2 + z % 2, (z // 2) * 8 + y * 2 + core)


def group_of(x, z):
    return x * 4 + (z % 2) * 2 + z // 2


def first_row(y):
    return pl.multiple_of(8 * ((5 * y) // 2), 8)


def columns(block, width):
    return pl.ds(pl.multiple_of(block * width, width), width)


def remote(src, dst, send, recv, to):
    return pltpu.make_async_remote_copy(
        src_ref=src, dst_ref=dst, send_sem=send, recv_sem=recv, device_id=to, device_id_type=MESH
    )


def loop(first, last, step):
    def run(i, carry):
        step(i)
        return carry

    lax.fori_loop(first, last, run, 0)


def each(first, last, step):
    for i in range(first, last):
        step(i)


class Near:
    def __init__(self):
        self.x, self.y, self.z, self.core = place()
        x, y, z, core = self.x, self.y, self.z, self.core
        self.dp = x * 2 + z % 2
        self.twin = z % 2
        self.a = x * (1 - core) + z * core
        self.b = x * core + z * (1 - core)
        self.mate = device(x, y, z, 1 - core)
        self.beside = device(x, y, z + 1 - 2 * (z % 2), core)
        xs, ys, zs = ([(at + k) % 4 for k in range(4)] for at in (x, y, z))
        self.xs = xs
        self.a_at = [jnp.where(core == 0, xs[k], zs[k]) for k in range(4)]
        self.b_at = [jnp.where(core == 0, zs[k], xs[k]) for k in range(4)]
        self.along_x = [device(xs[k], y, z, core) for k in range(4)]
        along_z = [device(x, y, zs[k], core) for k in range(4)]
        self.along_y = [device(x, ys[k], z, core) for k in range(4)]
        self.right, self.left = self.along_y[1], self.along_y[3]

        def choose(first, second):
            return [tuple(jnp.where(core == 0, p, q) for p, q in zip(one, two)) for one, two in zip(first, second)]

        self.along_a = choose(self.along_x, along_z)
        self.along_b = choose(along_z, self.along_x)
        other = [device(x, ys[k], z, 1 - core) for k in range(4)]
        self.line = [((self.along_y, other)[i % 2][i // 2], ys[i // 2], (core, 1 - core)[i % 2]) for i in range(8)]

    def group(self, a, b):
        return jnp.where(self.core == 0, a * 4 + (b % 2) * 2 + b // 2, b * 4 + (a % 2) * 2 + a // 2)

    def greet(self):
        barrier = pltpu.get_barrier_semaphore()

        def signal(to):
            pl.semaphore_signal(barrier, inc=1, device_id=to, device_id_type=MESH)

        each(1, 4, lambda k: signal(self.along_a[k]))
        each(1, 4, lambda k: signal(self.along_b[k]))
        each(1, 8, lambda i: signal(self.line[i][0]))

    def meet(self):
        pl.semaphore_wait(pltpu.get_barrier_semaphore(), 13)


def step_kernel(
    text_hbm, vision_hbm, text_states, vision_states, text_sum, vision_sum, text_out, vision_out,
    mine, other, paired, over_a, over_b, from_left, from_right, total, rest, first_in, first_sum, second_in, first_in_rest,
    first_sum_rest, second_in_rest, plane_rest, reduced,
    sums, rest_sums, windows, rest_windows, upper_own, upper_mid, upper_over, upper_from, lower_own, lower_in, lower_sum, cross_out, cross_in, lower_x,
    text_state, vision_raw, own_state, line_state, tile_state, dense, staged_rest, line_rest, packed, text_w, plane,
    load_sem, text_load, state_load, pair_s, pair_r, y_s, y_r, first_s, first_r, second_s, second_r,
    state_s, state_r, win_s, win_r, rest_win_s, rest_win_r, upper_s, upper_r, text_s, text_r, text2_s, text2_r,
    line_s, line_r, plane1_s, plane1_r, plane2_s, plane2_r, back_s, back_r, mate_s, mate_r, spread_s, spread_r,
    own_sem,
):
    near = Near()
    x, y, core = near.x, near.y, near.core
    up = UPPER * text_hbm.shape[0] // 16
    low = text_hbm.shape[0] - up
    upper_rows, lower_rows = pl.ds(0, up), pl.ds(up, low)
    blocks = [(y + 2) % 4, (y + 1) % 4, (y + 3) % 4, y, 4]
    order = (OPP, RIGHT, LEFT, REST, OWN)

    def loads(role):
        cols = columns(blocks[role], COLS)
        return (
            pltpu.make_async_copy(vision_hbm.at[1 - core, :, :, cols], other.at[role], load_sem.at[role, 0]),
            pltpu.make_async_copy(vision_hbm.at[core, :, :, cols], mine.at[role], load_sem.at[role, 1]),
        )

    def text_block(rows, block):
        return text_hbm.at[rows, columns(block, COLS)]

    def upper_load(q):
        return pltpu.make_async_copy(text_block(upper_rows, 2 * x + q), upper_own.at[q], text_load.at[q])

    def mid_load(q):
        return pltpu.make_async_copy(text_block(upper_rows, 2 * near.xs[1 + 2 * q] + q), upper_mid.at[q], text_load.at[6 + q])

    def lower_load(px):
        return pltpu.make_async_copy(text_block(lower_rows, 2 * px + near.twin), lower_own.at[px], text_load.at[2 + px])

    def state_copies(i):
        return (
            pltpu.make_async_copy(text_states[i], text_state.at[i], state_load.at[i, 0]),
            pltpu.make_async_copy(vision_states[i], vision_raw.at[i], state_load.at[i, 1]),
        )

    near.greet()
    for copy in loads(OPP):
        copy.start()
    for i in range(3):
        state_copies(i)[1].start()
    for role in order[1:]:
        for copy in loads(role):
            copy.start()
    each(0, 2, lambda q: upper_load(q).start())
    each(0, 2, lambda q: mid_load(q).start())
    each(0, 4, lambda px: lower_load(px).start())
    for i in range(3):
        state_copies(i)[0].start()

    near.meet()

    ahead, behind = near.along_x[1], near.along_x[3]

    def upper_copies():
        def go(src, dst, i, to):
            return remote(src, dst, upper_s.at[i], upper_r.at[i], to)

        def block(k, q):
            return text_block(upper_rows, 2 * near.xs[k] + q)

        return [
            go(block(2, 0), upper_over.at[0], 0, ahead),
            go(block(2, 1), upper_over.at[1], 1, behind),
            go(block(1, 1), upper_from.at[0, 1], 2, ahead),
            go(block(3, 0), upper_from.at[1, 0], 3, behind),
            go(upper_mid.at[0], upper_from.at[0, 0], 4, ahead),
            go(upper_mid.at[1], upper_from.at[1, 1], 5, behind),
        ]

    upper = upper_copies()

    def text_pass_on():
        each(0, 2, lambda q: mid_load(q).wait())
        for q in range(2):
            upper[q].wait_recv()

            def add(i, q=q):
                rows = pl.ds(pl.multiple_of(i * 32, 32), 32)
                upper_mid[q, rows] = upper_mid[q, rows] + upper_over[q, rows]

            loop(0, up // 32, add)
            upper[4 + q].start()

    def lower_copy(px):
        return remote(
            text_block(lower_rows, 2 * px + 1 - near.twin), lower_in.at[px], text_s.at[px], text_r.at[px],
            near.beside,
        )

    def pair(role, tile=None):
        cols = pl.ds(0, COLS) if tile is None else pl.ds(tile * TILE, TILE)
        src, dst = other.at[role, :, :, cols], paired.at[role, :, :, cols]
        return remote(src, dst, pair_s.at[role, tile or 0], pair_r.at[role, tile or 0], near.mate)

    def add_pair(role, tile):
        if tile == 0:
            loads(role)[1].wait()
        pair(role, tile).wait_recv()
        cols = slice(tile * TILE, (tile + 1) * TILE)

        def add(i):
            for j in range(4):
                g = 4 * i + j
                reduced[role, tile, g] = mine[role, g, :, cols] + paired[role, g, :, cols]

        loop(0, GROUPS // 4, add)

    def add_own():
        loads(OWN)[1].wait()
        pair(OWN).wait_recv()

        def add(i):
            for j in range(4):
                g = 4 * i + j
                both = mine[OWN, g] + paired[OWN, g]
                reduced[OWN, 0, g] = both[:, :TILE]
                reduced[OWN, 1, g] = both[:, TILE:]

        loop(0, GROUPS // 4, add)

    def add_rest():
        loads(REST)[1].wait()
        pair(REST).wait_recv()

        def add(i):
            a, b = i // 4, i % 4
            g = near.group(a, b)
            both = mine[REST, g] + paired[REST, g]
            rest[a, b, :ROWS] = both[:, :TILE]
            rest[a, b, ROWS:] = both[:, TILE:]

        each(0, GROUPS, add)

    half_a, half_b = pl.ds(0, 8), pl.ds(8, 8)

    def along(piece):
        tile, first, n = PIECES[piece]
        rows = pl.ds(first, n)

        def go(src, dst, i, to):
            return remote(src, dst, y_s.at[piece, i], y_r.at[piece, i], to)

        return [
            go(reduced.at[OPP, tile, half_a, rows], over_a.at[tile, :, rows], 0, near.right),
            go(reduced.at[OPP, tile, half_b, rows], over_b.at[tile, :, rows], 1, near.left),
            go(reduced.at[RIGHT, tile, half_b, rows], from_left.at[tile, half_b, rows], 2, near.right),
            go(reduced.at[LEFT, tile, half_a, rows], from_right.at[tile, half_a, rows], 3, near.left),
            go(reduced.at[RIGHT, tile, half_a, rows], from_left.at[tile, half_a, rows], 4, near.right),
            go(reduced.at[LEFT, tile, half_b, rows], from_right.at[tile, half_b, rows], 5, near.left),
        ]

    line = [along(piece) for piece in range(len(PIECES))]

    def pass_on(piece):
        tile, first, n = PIECES[piece]
        rows = pl.ds(first, n)
        line[piece][0].wait_recv()

        def add_a(i):
            for g in (2 * i, 2 * i + 1):
                reduced[RIGHT, tile, g, rows] = reduced[RIGHT, tile, g, rows] + over_a[tile, g, rows]

        loop(0, 4, add_a)
        line[piece][4].start()
        line[piece][1].wait_recv()

        def add_b(i):
            for g in (2 * i, 2 * i + 1):
                reduced[LEFT, tile, 8 + g, rows] = reduced[LEFT, tile, 8 + g, rows] + over_b[tile, g, rows]

        loop(0, 4, add_b)
        line[piece][5].start()

    def add_line(piece):
        tile, first, n = PIECES[piece]
        rows = pl.ds(first, n)
        for copy in line[piece][2:]:
            copy.wait_recv()

        def add(i):
            a, b = i // 4, i % 4
            g = near.group(a, b)
            total[tile, a, b, rows] = (
                reduced[OWN, tile, g, rows].astype(F32)
                + from_left[tile, g, rows].astype(F32)
                + from_right[tile, g, rows].astype(F32)
            ).astype(BF16)

        each(0, GROUPS, add)

    def pick(unit, of_rest, of_main):
        buffer, first, n = UNITS[unit]
        return of_rest if buffer == 0 else of_main.at[buffer - 1], pl.ds(first, n)

    def source(unit, a):
        ref, rows = pick(unit, rest, total)
        return ref.at[a, :, rows]

    def first_copy(unit, k):
        ref, rows = pick(unit, first_in_rest, first_in)
        return remote(
            source(unit, near.a_at[k]), ref.at[k, :, rows], first_s.at[unit, k], first_r.at[unit, k], near.along_a[k]
        )

    def second_copy(unit, k):
        src, rows = pick(unit, first_sum_rest, first_sum)
        dst, _ = pick(unit, second_in_rest, second_in)
        return remote(
            src.at[near.b_at[k], rows], dst.at[k, rows], second_s.at[unit, k], second_r.at[unit, k], near.along_b[k]
        )

    def first_step(unit):
        each(1, 4, lambda k: first_copy(unit, k).start())

    def second_step(unit):
        each(1, 4, lambda k: first_copy(unit, k).wait_recv())
        own = source(unit, near.a)
        got, rows = pick(unit, first_in_rest, first_in)
        made, _ = pick(unit, first_sum_rest, first_sum)

        def add(b):
            acc = own[b].astype(F32)
            for k in range(1, 4):
                acc = acc + got[k, b, rows].astype(F32)
            made[b, rows] = acc.astype(BF16)

        each(0, 4, add)
        each(1, 4, lambda k: second_copy(unit, k).start())

    def last_step(unit):
        each(1, 4, lambda k: second_copy(unit, k).wait_recv())
        made, rows = pick(unit, first_sum_rest, first_sum)
        got, _ = pick(unit, second_in_rest, second_in)
        acc = made[near.b, rows].astype(F32)
        for k in range(1, 4):
            acc = acc + got[k, rows].astype(F32)
        return acc

    def cross_copy():
        return remote(cross_out, cross_in, text2_s.at[0], text2_r.at[0], near.beside)

    def lower_x_copy(k):
        return remote(
            lower_sum.at[near.xs[k]], lower_x.at[k], text2_s.at[k], text2_r.at[k], near.along_x[k]
        )

    def text_middle():
        each(0, 2, lambda q: upper_load(q).wait())
        for copy in upper[2:]:
            copy.wait_recv()

        def add_upper(i):
            rows = pl.ds(pl.multiple_of(i * 32, 32), 32)

            def both(q):
                return upper_own[q, rows].astype(F32) + upper_from[0, q, rows].astype(F32) + upper_from[1, q, rows].astype(F32)

            cross_out[rows] = both(1 - near.twin).astype(BF16)
            text_sum[rows] = both(near.twin)

        loop(0, up // 32, add_upper)
        each(0, 4, lambda px: lower_load(px).wait())
        each(0, 4, lambda px: lower_copy(px).wait_recv())

        def add_lower(i):
            rows = pl.ds(pl.multiple_of(i * 32, 32), 32)
            for px in range(4):
                lower_sum[px, rows] = lower_own[px, rows] + lower_in[px, rows]

        loop(0, low // 32, add_lower)

    def text_cross():
        cross_copy().start()
        lower_x_copy(1).start()
        lower_x_copy(3).start()

    def text_weights(rows, grad):
        text_sum[rows] = grad
        text_w[rows] = adam_weights(grad, *[text_state[i, rows] for i in range(3)])

    def text_last():
        for i in range(3):
            state_copies(i)[0].wait()
        cross_copy().wait_recv()
        each(1, 4, lambda k: lower_x_copy(k).wait_recv())

        def add(i):
            rows = pl.ds(pl.multiple_of(i * 32, 32), 32)
            text_weights(rows, text_sum[rows] + cross_in[rows].astype(F32))

        def add_low(i):
            rows = pl.ds(pl.multiple_of(i * 32, 32), 32)
            acc = lower_own[x, rows].astype(F32) + lower_in[x, rows].astype(F32)
            for k in range(1, 4):
                acc = acc + lower_x[k, rows].astype(F32)
            text_weights(pl.ds(pl.multiple_of(up + i * 32, 32), 32), acc)

        loop(0, up // 32, add)
        loop(0, low // 32, add_low)

    def arrange_states():
        for i in range(3):
            state_copies(i)[1].wait()
        for layer in range(2):
            for i in range(3):
                for r in range(10):
                    own_state[layer, 10 * i + r : 10 * i + r + 1, :] = vision_raw[i, r, layer : layer + 1, :]

    def state_copy(i):
        to, py, pc = near.line[i]
        return remote(
            own_state.at[pc, :, columns(py, COLS)], line_state.at[y * 2 + core], state_s.at[i], state_r.at[i], to
        )

    def send_states():
        each(1, 8, lambda i: state_copy(i).start())
        line_state[y * 2 + core] = own_state[core, :, columns(y, COLS)]

    def join_states():
        each(1, 8, lambda i: state_copy(i).wait_recv())
        for place_on_line in range(8):
            for i in range(3):
                tile_state[i, 10 * place_on_line : 10 * place_on_line + 10, :] = line_state[
                    place_on_line, 10 * i : 10 * i + 10, :
                ]

    own_rows = pl.ds(first_row(y), 24)

    def win_copy(tile, i):
        to, py, _ = near.line[i]
        return remote(
            sums.at[tile, pl.ds(first_row(py), 24)], windows.at[core, 2 * y + tile], win_s.at[tile, i], win_r.at[tile, i],
            to,
        )

    def rest_win_copy(i):
        to, py, _ = near.line[i]
        return remote(
            rest_sums.at[:, pl.ds(first_row(py), 24)], rest_windows.at[core, y], rest_win_s.at[i], rest_win_r.at[i], to
        )

    def main_last(piece):
        tile, first, n = PIECES[piece]
        rows = pl.ds(first, n)
        grad = last_step(1 + piece)
        sums[tile, rows] = grad
        cols = slice(tile * TILE, (tile + 1) * TILE)
        plane[tile, near.a, near.b, rows] = adam_weights(grad, *[tile_state[i, rows, cols] for i in range(3)])
        each(1, 4, lambda k: plane1(1 + piece, k).start())

    def send_sums(tile):
        each(1, 8, lambda i: win_copy(tile, i).start())
        windows[core, 2 * y + tile] = sums[tile, own_rows]

    def rest_last():
        both = last_step(0)
        rest_sums[0] = both[:ROWS]
        rest_sums[1] = both[ROWS:]
        each(1, 8, lambda i: rest_win_copy(i).start())
        rest_windows[core, y] = rest_sums[:, own_rows]

    odd = y % 2 == 1

    def own_part(window):
        first = jnp.where(odd, window[4:14], window[0:10])
        second = jnp.where(odd, window[14:24], window[10:20])
        return jnp.where(core == 1, second, first)

    def line_rest_copy(i):
        to, _, pc = near.line[i]
        return remote(staged_rest.at[pc], line_rest.at[y * 2 + core], line_s.at[i], line_r.at[i], to)

    def owner_rest():
        each(1, 8, lambda i: rest_win_copy(i).wait_recv())
        for layer in range(2):
            for tile in range(2):
                cols = slice((8 + tile) * TILE, (9 + tile) * TILE)
                window = rest_windows[layer, 0, tile]
                for py in range(1, 4):
                    window = window + rest_windows[layer, py, tile]
                grad = own_part(window)
                dense[layer, 0:10, cols] = grad
                staged_rest[layer, tile, 0:10] = adam_weights(
                    grad, *[own_state[layer, 10 * i : 10 * i + 10, cols] for i in range(3)]
                )
        each(1, 8, lambda i: line_rest_copy(i).start())
        line_rest[y * 2 + core] = staged_rest[core]

    def owner_main(tile):
        each(1, 8, lambda i: win_copy(tile, i).wait_recv())
        for layer in range(2):
            for py in range(4):
                t = 2 * py + tile
                dense[layer, 0:10, t * TILE : (t + 1) * TILE] = own_part(windows[layer, t])

    def plane1(unit, k):
        ref, rows = pick(unit, plane_rest, plane)
        one = ref.at[near.a, near.b, rows]
        return remote(one, one, plane1_s.at[unit, k], plane1_r.at[unit, k], near.along_b[k])

    def plane2(unit, k):
        ref, rows = pick(unit, plane_rest, plane)
        row = ref.at[near.a, :, rows]
        return remote(row, row, plane2_s.at[unit, k], plane2_r.at[unit, k], near.along_a[k])

    def pack_rest():
        each(1, 8, lambda i: line_rest_copy(i).wait_recv())
        for tile in range(2):
            for i in range(8):
                packed[tile, 10 * i : 10 * i + 10, :] = line_rest[i, tile].astype(F32)[:10]
            plane_rest[near.a, near.b, tile * ROWS : (tile + 1) * ROWS] = packed[tile].astype(BF16)
        each(1, 4, lambda k: plane1(0, k).start())

    def across(unit):
        each(1, 4, lambda k: plane1(unit, k).wait_recv())
        each(1, 4, lambda k: plane2(unit, k).start())

    first_tile = {OPP: 2 * blocks[OPP], RIGHT: 2 * blocks[RIGHT], LEFT: 2 * blocks[LEFT], OWN: 2 * y, REST: 8}

    def held(role, tile):
        return vision_out.at[core, first_tile[role] + tile]

    def spread(unit):
        each(1, 4, lambda k: plane2(unit, k).wait_recv())
        buffer, first, n = UNITS[unit]
        rows = pl.ds(first, n)

        def move(i):
            a, b = i // 4, i % 4
            g = near.group(a, b)
            if buffer:
                vision_out[core, 2 * y + buffer - 1, g, rows] = plane[buffer - 1, a, b, rows]
            else:
                vision_out[core, 8, g] = plane_rest[a, b, :ROWS]
                vision_out[core, 9, g] = plane_rest[a, b, ROWS:]

        each(0, GROUPS, move)

    def back(piece):
        tile, first, n = PIECES[piece]
        rows = pl.ds(first, n)

        def go(role, half, i, to):
            part = held(role, tile).at[half, rows]
            return remote(part, part, back_s.at[piece, i], back_r.at[piece, i], to)

        nearer = [
            go(OWN, half_a, 0, near.right),
            go(OWN, half_b, 1, near.left),
            go(OWN, half_b, 2, near.right),
            go(OWN, half_a, 3, near.left),
        ]
        return nearer + [go(LEFT, half_a, 4, near.right), go(RIGHT, half_b, 5, near.left)]

    last = len(PIECES) - 1
    ways = [back(piece) for piece in range(len(PIECES))]

    def send_back(piece):
        spread(1 + piece)
        for copy in ways[piece][:4]:
            copy.start()
        give(OWN, piece)

    def forward(piece):
        ways[piece][0].wait_recv()
        ways[piece][4].start()
        ways[piece][1].wait_recv()
        ways[piece][5].start()

    def give_sides(piece):
        ways[piece][2].wait_recv()
        give(LEFT, piece)
        ways[piece][3].wait_recv()
        give(RIGHT, piece)

    def give_last(piece):
        ways[piece][4].wait_recv()
        ways[piece][5].wait_recv()
        give(OPP, piece)

    def mate(role, piece):
        if role == REST:
            part = held(role, piece)
        else:
            tile, first, n = PIECES[piece]
            part = held(role, tile).at[:, pl.ds(first, n)]
        return remote(part, part, mate_s.at[role, piece], mate_r.at[role, piece], near.mate)

    def give(role, piece):
        mate(role, piece).start()

    own_cols = columns(near.dp, COLS)

    def own_text():
        return pltpu.make_async_copy(text_w, text_out.at[:, own_cols], own_sem)

    def beside_copy():
        return remote(
            text_w.at[upper_rows], text_out.at[upper_rows, own_cols], spread_s.at[0, 0], spread_r.at[0, 0], near.beside
        )

    def x_copy(k):
        return remote(
            text_w.at[lower_rows], text_out.at[lower_rows, own_cols], spread_s.at[0, k], spread_r.at[0, k],
            near.along_x[k],
        )

    def upper_ways():
        def go(block, i, to):
            part = text_out.at[upper_rows, columns(block, COLS)]
            return remote(part, part, spread_s.at[1, i], spread_r.at[1, i], to)

        return [
            go(2 * x, 0, ahead),
            go(2 * x + 1, 1, behind),
            go(2 * x + 1, 2, ahead),
            go(2 * x, 3, behind),
            go(2 * near.xs[3], 4, ahead),
            go(2 * near.xs[1] + 1, 5, behind),
        ]

    upper_on = upper_ways()

    def text_spread_last():
        for i in range(2):
            upper_on[i].wait_recv()
            upper_on[4 + i].start()

    def lower_on(px):
        one = text_out.at[lower_rows, columns(2 * px + near.twin, COLS)]
        return remote(one, one, spread_s.at[2, px], spread_r.at[2, px], near.beside)

    def text_spread():
        own_text().start()
        beside_copy().start()
        x_copy(1).start()
        x_copy(3).start()

    def text_spread_on():
        own_text().wait()
        beside_copy().wait_recv()
        for copy in upper_on[:4]:
            copy.start()
        each(1, 4, lambda k: x_copy(k).wait_recv())
        each(0, 4, lambda px: lower_on(px).start())

    def start_pair(role, tile=None):
        if not tile:
            loads(role)[0].wait()
        pair(role, tile).start()

    start_pair(OPP, 0)
    start_pair(RIGHT, 0)
    add_pair(OPP, 0)
    line[0][0].start()
    line[0][1].start()
    start_pair(LEFT, 0)
    for copy in upper[:4]:
        copy.start()
    each(0, 4, lambda px: lower_copy(px).start())
    add_pair(RIGHT, 0)
    line[0][2].start()
    line[1][0].start()
    start_pair(REST)
    add_pair(LEFT, 0)
    line[0][3].start()
    line[1][1].start()
    start_pair(OWN)
    for role in (OPP, RIGHT, LEFT):
        start_pair(role, 1)
    add_rest()
    first_step(0)
    pass_on(0)
    line[1][2].start()
    line[1][3].start()
    add_own()
    arrange_states()
    text_pass_on()
    pass_on(1)
    send_states()
    for role in (OPP, RIGHT, LEFT):
        add_pair(role, 1)
    for copy in line[2][:4] + line[3][:4]:
        copy.start()
    add_line(0)
    first_step(1)
    text_middle()
    add_line(1)
    first_step(2)
    second_step(1)
    text_cross()
    pass_on(2)
    second_step(0)
    second_step(2)
    lower_x_copy(2).start()
    join_states()
    main_last(0)
    pass_on(3)
    rest_last()
    main_last(1)
    across(1)
    send_sums(0)
    add_line(2)
    first_step(3)
    across(2)
    owner_rest()
    send_back(0)
    add_line(3)
    first_step(4)
    second_step(3)
    text_last()
    text_spread()
    send_back(1)
    forward(0)
    second_step(4)
    x_copy(2).start()
    main_last(2)
    pack_rest()
    main_last(3)
    across(3)
    forward(1)
    across(4)
    across(0)
    send_back(2)
    text_spread_on()
    send_back(3)
    send_sums(1)
    give_sides(0)
    give_last(0)
    give_sides(1)
    give_last(1)
    forward(2)
    forward(3)
    text_spread_last()
    spread(0)
    give(REST, 0)
    give(REST, 1)
    give_sides(2)
    give_last(2)
    owner_main(0)
    owner_main(1)
    for r in range(10):
        for layer in range(2):
            vision_sum[r, layer : layer + 1, :] = dense[layer, r : r + 1, :]

    for role in (OPP, RIGHT, LEFT):
        for tile in range(2):
            pair(role, tile).wait_send()
    for role in (REST, OWN):
        pair(role).wait_send()
    for copies in line:
        for copy in copies:
            copy.wait_send()
    for copy in upper:
        copy.wait_send()
    each(0, 4, lambda px: lower_copy(px).wait_send())
    cross_copy().wait_send()
    each(1, 4, lambda k: lower_x_copy(k).wait_send())
    for unit in range(len(UNITS)):
        for copies in (first_copy, second_copy, plane1, plane2):
            each(1, 4, lambda k: copies(unit, k).wait_send())
    each(1, 8, lambda i: state_copy(i).wait_send())
    each(1, 8, lambda i: rest_win_copy(i).wait_send())
    for tile in range(2):
        each(1, 8, lambda i: win_copy(tile, i).wait_send())
    each(1, 8, lambda i: line_rest_copy(i).wait_send())
    beside_copy().wait_send()
    each(1, 4, lambda k: x_copy(k).wait_send())

    give_sides(3)
    give_last(3)
    for copy in upper_on[2:]:
        copy.wait_recv()
    for copy in upper_on:
        copy.wait_send()
    each(0, 4, lambda px: lower_on(px).wait())
    for copies in ways:
        for copy in copies:
            copy.wait_send()
    for role in range(5):
        for piece in range(2 if role == REST else len(PIECES)):
            mate(role, piece).wait()


def kernel_of(given):
    def run(text_hbm, vision_hbm, *refs):
        given(text_hbm, vision_hbm, refs[:3], refs[3:6], *refs[6:])

    return run


def step(text, vision, text_states, vision_states):
    rows = text.shape[0]
    up = UPPER * rows // 16
    low = rows - up
    block = (GROUPS, ROWS, COLS)
    tile = (GROUPS, ROWS, TILE)
    square = (4, 4, ROWS, TILE)
    dma = pltpu.SemaphoreType.DMA
    vmem = pltpu.VMEM
    return pl.pallas_call(
        kernel_of(step_kernel),
        name="sum_step_gather",
        out_shape=(
            jax.ShapeDtypeStruct((rows, COLS), F32),
            jax.ShapeDtypeStruct(vision_states[0].shape, F32),
            jax.ShapeDtypeStruct((rows, 8 * COLS), BF16),
            jax.ShapeDtypeStruct((2, 10) + tile, BF16),
        ),
        in_specs=[pl.BlockSpec(memory_space=pltpu.HBM)] * 8,
        out_specs=[pl.BlockSpec(memory_space=pltpu.VMEM)] * 4,
        scratch_shapes=[
            vmem((5,) + block, BF16),
            vmem((5,) + block, BF16),
            vmem((5,) + block, BF16),
            vmem((2, 8, ROWS, TILE), BF16),
            vmem((2, 8, ROWS, TILE), BF16),
            vmem((2,) + tile, BF16),
            vmem((2,) + tile, BF16),
            vmem((2,) + square, BF16),
            vmem((4, 4, 2 * ROWS, TILE), BF16),
            vmem((2,) + square, BF16),
            vmem((2, 4, ROWS, TILE), BF16),
            vmem((2, 4, ROWS, TILE), BF16),
            vmem((4, 4, 2 * ROWS, TILE), BF16),
            vmem((4, 2 * ROWS, TILE), BF16),
            vmem((4, 2 * ROWS, TILE), BF16),
            vmem((4, 4, 2 * ROWS, TILE), BF16),
            vmem((4, 2) + tile, BF16),
            vmem((2, ROWS, TILE), F32),
            vmem((2, ROWS, TILE), F32),
            vmem((2, 8, 24, TILE), F32),
            vmem((2, 4, 2, 24, TILE), F32),
            vmem((2, up, COLS), BF16),
            vmem((2, up, COLS), BF16),
            vmem((2, up, COLS), BF16),
            vmem((2, 2, up, COLS), BF16),
            vmem((4, low, COLS), BF16),
            vmem((4, low, COLS), BF16),
            vmem((4, low, COLS), BF16),
            vmem((up, COLS), BF16),
            vmem((up, COLS), BF16),
            vmem((4, low, COLS), BF16),
            vmem((3, rows, COLS), F32),
            vmem((3,) + vision_states[0].shape, F32),
            vmem((2, 32, 5 * COLS), F32),
            vmem((8, 32, COLS), F32),
            vmem((3, ROWS, COLS), F32),
            vmem((2, 16, 5 * COLS), F32),
            vmem((2, 2, 16, TILE), BF16),
            vmem((8, 2, 16, TILE), BF16),
            vmem((2, ROWS, TILE), F32),
            vmem((rows, COLS), BF16),
            vmem((2,) + square, BF16),
            dma((5, 2)),
            dma((8,)),
            dma((3, 2)),
            dma((5, 2)), dma((5, 2)),
            dma((4, 6)), dma((4, 6)),
            dma((6, 4)), dma((6, 4)),
            dma((6, 4)), dma((6, 4)),
            dma((8,)), dma((8,)),
            dma((2, 8)), dma((2, 8)),
            dma((8,)), dma((8,)),
            dma((6,)), dma((6,)),
            dma((4,)), dma((4,)),
            dma((4,)), dma((4,)),
            dma((8,)), dma((8,)),
            dma((6, 4)), dma((6, 4)),
            dma((6, 4)), dma((6, 4)),
            dma((4, 6)), dma((4, 6)),
            dma((5, 4)), dma((5, 4)),
            dma((3, 6)), dma((3, 6)),
            dma,
        ],
        compiler_params=pltpu.CompilerParams(collective_id=1, has_side_effects=True, vmem_limit_bytes=40 << 20),
    )(*[pltpu.with_memory_space_constraint(array, pltpu.HBM) for array in (text, vision, *text_states, *vision_states)])


def finish_kernel(*refs):
    text, vision, text_full, vision_full = refs[:5], refs[5:10], refs[10], refs[11]
    outs, vision_w = refs[12:22], refs[21]
    text_made, vision_made, sem, tile_sem = refs[22:]
    text_w = outs[4]
    copies = [
        pltpu.make_async_copy(vision_full.at[layer, t], vision_w.at[layer, :, :, t * TILE : (t + 1) * TILE], tile_sem.at[layer, t])
        for layer in range(2)
        for t in range(10)
    ]
    copies.append(pltpu.make_async_copy(text_full, text_w, sem.at[1]))
    for copy in copies:
        copy.start()

    def one(i):
        rows = pl.ds(pl.multiple_of(i * 32, 32), 32)
        made = adam_step(*[ref[rows] for ref in text])
        for j in range(4):
            text_made[j, rows] = made[j]

    loop(0, text_made.shape[1] // 32, one)
    for j in range(4):
        copies.append(pltpu.make_async_copy(text_made.at[j], outs[j], sem.at[2 + j]))
        copies[-1].start()

    def row(r):
        made = adam_step(*[ref[r] for ref in vision])
        for j in range(4):
            vision_made[j, r] = made[j]

    loop(0, vision_made.shape[1], row)
    for j in range(4):
        copies.append(pltpu.make_async_copy(vision_made.at[j], outs[5 + j], sem.at[6 + j]))
        copies[-1].start()
    for copy in copies:
        copy.wait()


def finish(text, vision, text_full, vision_full):
    def like(array):
        return jax.ShapeDtypeStruct(array.shape, array.dtype)

    in_hbm, in_vmem = pl.BlockSpec(memory_space=pltpu.HBM), pl.BlockSpec(memory_space=pltpu.VMEM)
    return pl.pallas_call(
        finish_kernel,
        name="write_results",
        out_shape=(like(text[0]),) * 4
        + (like(text_full),)
        + (like(vision[0]),) * 4
        + (jax.ShapeDtypeStruct((2, GROUPS, ROWS, 5 * COLS), BF16),),
        in_specs=[in_vmem] * 10 + [in_hbm] * 2,
        out_specs=[in_hbm] * 10,
        scratch_shapes=[
            pltpu.VMEM((4,) + text[0].shape, F32),
            pltpu.VMEM((4,) + vision[0].shape, F32),
            pltpu.SemaphoreType.DMA((10,)),
            pltpu.SemaphoreType.DMA((2, 10)),
        ],
        compiler_params=pltpu.CompilerParams(vmem_limit_bytes=16 << 20),
    )(*text, *vision, text_full, vision_full)


def body(
    text_grads, text_master, text_moment, text_second, text_ref,
    vision_grads, vision_master, vision_moment, vision_second, vision_ref,
):
    layers, width = vision_grads.shape[1], vision_grads.shape[3]
    text_states = (text_moment, text_second, text_master, text_ref)
    vision_states = tuple(
        jnp.transpose(array, (1, 0, 2)) for array in (vision_moment, vision_second, vision_master, vision_ref)
    )
    text_total, vision_total, text_full, vision_full = step(
        text_grads[0], vision_grads.reshape(layers, GROUPS, ROWS, width), text_states[:3], vision_states[:3]
    )
    outs = finish((text_total,) + text_states, (vision_total,) + vision_states, text_full, vision_full)
    vision_out = tuple(jnp.transpose(array, (1, 0, 2)) for array in outs[5:9])
    return outs[:5] + vision_out + (outs[9].reshape(layers, width, width),)


def solution(mesh):
    owned = P("tensor", "dp")
    vision_owned = P(None, ("dp", "tensor"), None)
    return jax.shard_map(
        body,
        mesh=mesh,
        in_specs=(P("dp", "tensor", None),) + (owned,) * 4 + (P(("dp", "tensor"), None, None, None),) + (vision_owned,) * 4,
        out_specs=(owned,) * 4 + (P("tensor", None),) + (vision_owned,) * 4 + (P(),),
        check_vma=False,
    )
```

```python
import functools

import jax
import jax.numpy as jnp
from jax import lax
from jax.experimental import pallas as pl
from jax.experimental.pallas import tpu as pltpu
from jax.sharding import PartitionSpec as P

MESH = pl.DeviceIdType.MESH
BF16, F32 = jnp.bfloat16, jnp.float32

beta_one = 0.9
beta_two = 0.95
correct_one = 1.0 - 0.9**10
correct_two = 1.0 - 0.95**10
learn_rate = 0.01
decay_rate = 0.1
blend_rate = 0.6

GROUPS = 16
ROWS = 80
TILE = 128
UPPER = 9
COLS = 2 * TILE
OPP, RIGHT, LEFT, OWN, REST = range(5)
PIECES = ((0, 0, 32), (0, 32, 48), (1, 0, 48), (1, 48, 32))
UNITS = ((0, 0, 2 * ROWS),) + tuple((1 + tile, first, n) for tile, first, n in PIECES)


def adam_step(grad, moment, second, master, refcopy):
    moment_new = beta_one * moment + (1.0 - beta_one) * grad
    second_new = beta_two * second + (1.0 - beta_two) * grad * grad
    update = moment_new / correct_one / (jnp.sqrt(second_new / correct_two) + 1e-08)
    master_new = master - learn_rate * (update + decay_rate * master)
    ref_new = blend_rate * master_new + (1.0 - blend_rate) * refcopy
    return (master_new, moment_new, second_new, ref_new, master_new.astype(BF16))


def adam_weights(grad, moment, second, master):
    return adam_step(grad, moment, second, master, master)[4]


def place():
    dp, tensor = lax.axis_index("dp"), lax.axis_index("tensor")
    x = dp // 2
    z = (tensor // 8) * 2 + dp % 2
    y = (tensor % 8) // 2
    return x, y, z, tensor % 2


def device(x, y, z, core):
    return (x * 2 + z % 2, (z // 2) * 8 + y * 2 + core)


def group_of(x, z):
    return x * 4 + (z % 2) * 2 + z // 2


def first_row(y):
    return pl.multiple_of(8 * ((5 * y) // 2), 8)


def columns(block, width):
    return pl.ds(pl.multiple_of(block * width, width), width)


def remote(src, dst, send, recv, to):
    return pltpu.make_async_remote_copy(
        src_ref=src, dst_ref=dst, send_sem=send, recv_sem=recv, device_id=to, device_id_type=MESH
    )


def loop(first, last, step):
    def run(i, carry):
        step(i)
        return carry

    lax.fori_loop(first, last, run, 0)


def each(first, last, step):
    for i in range(first, last):
        step(i)


class Near:
    def __init__(self):
        self.x, self.y, self.z, self.core = place()
        x, y, z, core = self.x, self.y, self.z, self.core
        self.dp = x * 2 + z % 2
        self.twin = z % 2
        self.a = x * (1 - core) + z * core
        self.b = x * core + z * (1 - core)
        self.mate = device(x, y, z, 1 - core)
        self.beside = device(x, y, z + 1 - 2 * (z % 2), core)
        xs, ys, zs = ([(at + k) % 4 for k in range(4)] for at in (x, y, z))
        self.xs = xs
        self.a_at = [jnp.where(core == 0, xs[k], zs[k]) for k in range(4)]
        self.b_at = [jnp.where(core == 0, zs[k], xs[k]) for k in range(4)]
        self.along_x = [device(xs[k], y, z, core) for k in range(4)]
        along_z = [device(x, y, zs[k], core) for k in range(4)]
        self.along_y = [device(x, ys[k], z, core) for k in range(4)]
        self.right, self.left = self.along_y[1], self.along_y[3]

        def choose(first, second):
            return [tuple(jnp.where(core == 0, p, q) for p, q in zip(one, two)) for one, two in zip(first, second)]

        self.along_a = choose(self.along_x, along_z)
        self.along_b = choose(along_z, self.along_x)
        other = [device(x, ys[k], z, 1 - core) for k in range(4)]
        self.line = [((self.along_y, other)[i % 2][i // 2], ys[i // 2], (core, 1 - core)[i % 2]) for i in range(8)]

    def group(self, a, b):
        return jnp.where(self.core == 0, a * 4 + (b % 2) * 2 + b // 2, b * 4 + (a % 2) * 2 + a // 2)

    def greet(self):
        barrier = pltpu.get_barrier_semaphore()

        def signal(to):
            pl.semaphore_signal(barrier, inc=1, device_id=to, device_id_type=MESH)

        each(1, 4, lambda k: signal(self.along_a[k]))
        each(1, 4, lambda k: signal(self.along_b[k]))
        each(1, 8, lambda i: signal(self.line[i][0]))

    def meet(self):
        pl.semaphore_wait(pltpu.get_barrier_semaphore(), 13)


def step_kernel(
    text_hbm, vision_hbm, text_states, vision_states, text_sum, vision_sum, text_out, vision_out,
    mine, other, paired, over_a, over_b, from_left, from_right, total, rest, first_in, first_sum, second_in, first_in_rest,
    first_sum_rest, second_in_rest, plane_rest, reduced,
    sums, rest_sums, windows, rest_windows, upper_own, upper_mid, upper_over, upper_from, lower_own, lower_in, lower_sum, cross_out, cross_in, lower_x,
    text_state, vision_raw, own_state, line_state, tile_state, dense, staged_rest, line_rest, packed, text_w, plane,
    load_sem, text_load, state_load, pair_s, pair_r, y_s, y_r, first_s, first_r, second_s, second_r,
    state_s, state_r, win_s, win_r, rest_win_s, rest_win_r, upper_s, upper_r, text_s, text_r, text2_s, text2_r,
    line_s, line_r, plane1_s, plane1_r, plane2_s, plane2_r, back_s, back_r, mate_s, mate_r, spread_s, spread_r,
    own_sem,
):
    near = Near()
    x, y, core = near.x, near.y, near.core
    up = UPPER * text_hbm.shape[0] // 16
    low = text_hbm.shape[0] - up
    upper_rows, lower_rows = pl.ds(0, up), pl.ds(up, low)
    blocks = [(y + 2) % 4, (y + 1) % 4, (y + 3) % 4, y, 4]
    order = (OPP, RIGHT, LEFT, REST, OWN)

    def loads(role):
        cols = columns(blocks[role], COLS)
        return (
            pltpu.make_async_copy(vision_hbm.at[1 - core, :, :, cols], other.at[role], load_sem.at[role, 0]),
            pltpu.make_async_copy(vision_hbm.at[core, :, :, cols], mine.at[role], load_sem.at[role, 1]),
        )

    def text_block(rows, block):
        return text_hbm.at[rows, columns(block, COLS)]

    def upper_load(q):
        return pltpu.make_async_copy(text_block(upper_rows, 2 * x + q), upper_own.at[q], text_load.at[q])

    def mid_load(q):
        return pltpu.make_async_copy(text_block(upper_rows, 2 * near.xs[1 + 2 * q] + q), upper_mid.at[q], text_load.at[6 + q])

    def lower_load(px):
        return pltpu.make_async_copy(text_block(lower_rows, 2 * px + near.twin), lower_own.at[px], text_load.at[2 + px])

    def state_copies(i):
        return (
            pltpu.make_async_copy(text_states[i], text_state.at[i], state_load.at[i, 0]),
            pltpu.make_async_copy(vision_states[i], vision_raw.at[i], state_load.at[i, 1]),
        )

    near.greet()
    for copy in loads(OPP):
        copy.start()
    for i in range(3):
        state_copies(i)[1].start()
    for role in order[1:]:
        for copy in loads(role):
            copy.start()
    each(0, 2, lambda q: upper_load(q).start())
    each(0, 2, lambda q: mid_load(q).start())
    each(0, 4, lambda px: lower_load(px).start())
    for i in range(3):
        state_copies(i)[0].start()

    near.meet()

    ahead, behind = near.along_x[1], near.along_x[3]

    def upper_copies():
        def go(src, dst, i, to):
            return remote(src, dst, upper_s.at[i], upper_r.at[i], to)

        def block(k, q):
            return text_block(upper_rows, 2 * near.xs[k] + q)

        return [
            go(block(2, 0), upper_over.at[0], 0, ahead),
            go(block(2, 1), upper_over.at[1], 1, behind),
            go(block(1, 1), upper_from.at[0, 1], 2, ahead),
            go(block(3, 0), upper_from.at[1, 0], 3, behind),
            go(upper_mid.at[0], upper_from.at[0, 0], 4, ahead),
            go(upper_mid.at[1], upper_from.at[1, 1], 5, behind),
        ]

    upper = upper_copies()

    def text_pass_on():
        each(0, 2, lambda q: mid_load(q).wait())
        for q in range(2):
            upper[q].wait_recv()

            def add(i, q=q):
                rows = pl.ds(pl.multiple_of(i * 32, 32), 32)
                upper_mid[q, rows] = upper_mid[q, rows] + upper_over[q, rows]

            loop(0, up // 32, add)
            upper[4 + q].start()

    def lower_copy(px):
        return remote(
            text_block(lower_rows, 2 * px + 1 - near.twin), lower_in.at[px], text_s.at[px], text_r.at[px],
            near.beside,
        )

    def pair(role, tile=None):
        cols = pl.ds(0, COLS) if tile is None else pl.ds(tile * TILE, TILE)
        src, dst = other.at[role, :, :, cols], paired.at[role, :, :, cols]
        return remote(src, dst, pair_s.at[role, tile or 0], pair_r.at[role, tile or 0], near.mate)

    def add_pair(role, tile):
        if tile == 0:
            loads(role)[1].wait()
        pair(role, tile).wait_recv()
        cols = slice(tile * TILE, (tile + 1) * TILE)

        def add(i):
            for j in range(4):
                g = 4 * i + j
                reduced[role, tile, g] = mine[role, g, :, cols] + paired[role, g, :, cols]

        loop(0, GROUPS // 4, add)

    def add_own():
        loads(OWN)[1].wait()
        pair(OWN).wait_recv()

        def add(i):
            for j in range(4):
                g = 4 * i + j
                both = mine[OWN, g] + paired[OWN, g]
                reduced[OWN, 0, g] = both[:, :TILE]
                reduced[OWN, 1, g] = both[:, TILE:]

        loop(0, GROUPS // 4, add)

    def add_rest():
        loads(REST)[1].wait()
        pair(REST).wait_recv()

        def add(i):
            a, b = i // 4, i % 4
            g = near.group(a, b)
            both = mine[REST, g] + paired[REST, g]
            rest[a, b, :ROWS] = both[:, :TILE]
            rest[a, b, ROWS:] = both[:, TILE:]

        each(0, GROUPS, add)

    half_a, half_b = pl.ds(0, 8), pl.ds(8, 8)

    def along(piece):
        tile, first, n = PIECES[piece]
        rows = pl.ds(first, n)

        def go(src, dst, i, to):
            return remote(src, dst, y_s.at[piece, i], y_r.at[piece, i], to)

        return [
            go(reduced.at[OPP, tile, half_a, rows], over_a.at[tile, :, rows], 0, near.right),
            go(reduced.at[OPP, tile, half_b, rows], over_b.at[tile, :, rows], 1, near.left),
            go(reduced.at[RIGHT, tile, half_b, rows], from_left.at[tile, half_b, rows], 2, near.right),
            go(reduced.at[LEFT, tile, half_a, rows], from_right.at[tile, half_a, rows], 3, near.left),
            go(reduced.at[RIGHT, tile, half_a, rows], from_left.at[tile, half_a, rows], 4, near.right),
            go(reduced.at[LEFT, tile, half_b, rows], from_right.at[tile, half_b, rows], 5, near.left),
        ]

    line = [along(piece) for piece in range(len(PIECES))]

    def pass_on(piece):
        tile, first, n = PIECES[piece]
        rows = pl.ds(first, n)
        line[piece][0].wait_recv()

        def add_a(i):
            for g in (2 * i, 2 * i + 1):
                reduced[RIGHT, tile, g, rows] = reduced[RIGHT, tile, g, rows] + over_a[tile, g, rows]

        loop(0, 4, add_a)
        line[piece][4].start()
        line[piece][1].wait_recv()

        def add_b(i):
            for g in (2 * i, 2 * i + 1):
                reduced[LEFT, tile, 8 + g, rows] = reduced[LEFT, tile, 8 + g, rows] + over_b[tile, g, rows]

        loop(0, 4, add_b)
        line[piece][5].start()

    def add_line(piece):
        tile, first, n = PIECES[piece]
        rows = pl.ds(first, n)
        for copy in line[piece][2:]:
            copy.wait_recv()

        def add(i):
            a, b = i // 4, i % 4
            g = near.group(a, b)
            total[tile, a, b, rows] = (
                reduced[OWN, tile, g, rows].astype(F32)
                + from_left[tile, g, rows].astype(F32)
                + from_right[tile, g, rows].astype(F32)
            ).astype(BF16)

        each(0, GROUPS, add)

    def pick(unit, of_rest, of_main):
        buffer, first, n = UNITS[unit]
        return of_rest if buffer == 0 else of_main.at[buffer - 1], pl.ds(first, n)

    def source(unit, a):
        ref, rows = pick(unit, rest, total)
        return ref.at[a, :, rows]

    def first_copy(unit, k):
        ref, rows = pick(unit, first_in_rest, first_in)
        return remote(
            source(unit, near.a_at[k]), ref.at[k, :, rows], first_s.at[unit, k], first_r.at[unit, k], near.along_a[k]
        )

    def second_copy(unit, k):
        src, rows = pick(unit, first_sum_rest, first_sum)
        dst, _ = pick(unit, second_in_rest, second_in)
        return remote(
            src.at[near.b_at[k], rows], dst.at[k, rows], second_s.at[unit, k], second_r.at[unit, k], near.along_b[k]
        )

    def first_step(unit):
        each(1, 4, lambda k: first_copy(unit, k).start())

    def second_step(unit):
        each(1, 4, lambda k: first_copy(unit, k).wait_recv())
        own = source(unit, near.a)
        got, rows = pick(unit, first_in_rest, first_in)
        made, _ = pick(unit, first_sum_rest, first_sum)

        def add(b):
            acc = own[b].astype(F32)
            for k in range(1, 4):
                acc = acc + got[k, b, rows].astype(F32)
            made[b, rows] = acc.astype(BF16)

        each(0, 4, add)
        each(1, 4, lambda k: second_copy(unit, k).start())

    def last_step(unit):
        each(1, 4, lambda k: second_copy(unit, k).wait_recv())
        made, rows = pick(unit, first_sum_rest, first_sum)
        got, _ = pick(unit, second_in_rest, second_in)
        acc = made[near.b, rows].astype(F32)
        for k in range(1, 4):
            acc = acc + got[k, rows].astype(F32)
        return acc

    def cross_copy():
        return remote(cross_out, cross_in, text2_s.at[0], text2_r.at[0], near.beside)

    def lower_x_copy(k):
        return remote(
            lower_sum.at[near.xs[k]], lower_x.at[k], text2_s.at[k], text2_r.at[k], near.along_x[k]
        )

    def text_middle():
        each(0, 2, lambda q: upper_load(q).wait())
        for copy in upper[2:]:
            copy.wait_recv()

        def add_upper(i):
            rows = pl.ds(pl.multiple_of(i * 32, 32), 32)

            def both(q):
                return upper_own[q, rows].astype(F32) + upper_from[0, q, rows].astype(F32) + upper_from[1, q, rows].astype(F32)

            cross_out[rows] = both(1 - near.twin).astype(BF16)
            text_sum[rows] = both(near.twin)

        loop(0, up // 32, add_upper)
        each(0, 4, lambda px: lower_load(px).wait())
        each(0, 4, lambda px: lower_copy(px).wait_recv())

        def add_lower(i):
            rows = pl.ds(pl.multiple_of(i * 32, 32), 32)
            for px in range(4):
                lower_sum[px, rows] = lower_own[px, rows] + lower_in[px, rows]

        loop(0, low // 32, add_lower)

    def text_cross():
        cross_copy().start()
        lower_x_copy(1).start()
        lower_x_copy(3).start()

    def text_weights(rows, grad):
        text_sum[rows] = grad
        text_w[rows] = adam_weights(grad, *[text_state[i, rows] for i in range(3)])

    def text_last():
        for i in range(3):
            state_copies(i)[0].wait()
        cross_copy().wait_recv()
        each(1, 4, lambda k: lower_x_copy(k).wait_recv())

        def add(i):
            rows = pl.ds(pl.multiple_of(i * 32, 32), 32)
            text_weights(rows, text_sum[rows] + cross_in[rows].astype(F32))

        def add_low(i):
            rows = pl.ds(pl.multiple_of(i * 32, 32), 32)
            acc = lower_own[x, rows].astype(F32) + lower_in[x, rows].astype(F32)
            for k in range(1, 4):
                acc = acc + lower_x[k, rows].astype(F32)
            text_weights(pl.ds(pl.multiple_of(up + i * 32, 32), 32), acc)

        loop(0, up // 32, add)
        loop(0, low // 32, add_low)

    def arrange_states():
        for i in range(3):
            state_copies(i)[1].wait()
        for layer in range(2):
            for i in range(3):
                for r in range(10):
                    own_state[layer, 10 * i + r : 10 * i + r + 1, :] = vision_raw[i, r, layer : layer + 1, :]

    def state_copy(i):
        to, py, pc = near.line[i]
        return remote(
            own_state.at[pc, pl.ds(0, 32), columns(py, COLS)], line_state.at[y * 2 + core, pl.ds(0, 32)], state_s.at[i],
            state_r.at[i], to,
        )

    def send_states():
        each(1, 8, lambda i: state_copy(i).start())
        line_state[y * 2 + core, :32] = own_state[core, :32, columns(y, COLS)]

    def join_states():
        each(1, 8, lambda i: state_copy(i).wait_recv())
        for place_on_line in range(8):
            for i in range(3):
                tile_state[i, 10 * place_on_line : 10 * place_on_line + 10, :] = line_state[
                    place_on_line, 10 * i : 10 * i + 10, :
                ]

    own_rows = pl.ds(first_row(y), 24)

    def win_copy(tile, i):
        to, py, _ = near.line[i]
        return remote(
            sums.at[tile, pl.ds(first_row(py), 24)], windows.at[core, 2 * y + tile], win_s.at[tile, i], win_r.at[tile, i],
            to,
        )

    def rest_win_copy(i):
        to, py, _ = near.line[i]
        return remote(
            rest_sums.at[:, pl.ds(first_row(py), 24)], rest_windows.at[core, y], rest_win_s.at[i], rest_win_r.at[i], to
        )

    def main_last(piece):
        tile, first, n = PIECES[piece]
        rows = pl.ds(first, n)
        grad = last_step(1 + piece)
        sums[tile, rows] = grad
        cols = slice(tile * TILE, (tile + 1) * TILE)
        plane[tile, near.a, near.b, rows] = adam_weights(grad, *[tile_state[i, rows, cols] for i in range(3)])
        each(1, 4, lambda k: plane1(1 + piece, k).start())

    def send_sums(tile):
        each(1, 8, lambda i: win_copy(tile, i).start())
        windows[core, 2 * y + tile] = sums[tile, own_rows]

    def rest_last():
        both = last_step(0)
        rest_sums[0] = both[:ROWS]
        rest_sums[1] = both[ROWS:]
        each(1, 8, lambda i: rest_win_copy(i).start())
        rest_windows[core, y] = rest_sums[:, own_rows]

    odd = y % 2 == 1

    def own_part(window):
        first = jnp.where(odd, window[4:14], window[0:10])
        second = jnp.where(odd, window[14:24], window[10:20])
        return jnp.where(core == 1, second, first)

    def line_rest_copy(i):
        to, _, pc = near.line[i]
        return remote(staged_rest.at[pc], line_rest.at[y * 2 + core], line_s.at[i], line_r.at[i], to)

    def owner_rest():
        each(1, 8, lambda i: rest_win_copy(i).wait_recv())
        for layer in range(2):
            for tile in range(2):
                cols = slice((8 + tile) * TILE, (9 + tile) * TILE)
                window = rest_windows[layer, 0, tile]
                for py in range(1, 4):
                    window = window + rest_windows[layer, py, tile]
                grad = own_part(window)
                dense[layer, 0:10, cols] = grad
                staged_rest[layer, tile, 0:10] = adam_weights(
                    grad, *[own_state[layer, 10 * i : 10 * i + 10, cols] for i in range(3)]
                )
        each(1, 8, lambda i: line_rest_copy(i).start())
        line_rest[y * 2 + core] = staged_rest[core]

    def owner_main(tile):
        each(1, 8, lambda i: win_copy(tile, i).wait_recv())
        for layer in range(2):
            for py in range(4):
                t = 2 * py + tile
                dense[layer, 0:10, t * TILE : (t + 1) * TILE] = own_part(windows[layer, t])

    def plane1(unit, k):
        ref, rows = pick(unit, plane_rest, plane)
        one = ref.at[near.a, near.b, rows]
        return remote(one, one, plane1_s.at[unit, k], plane1_r.at[unit, k], near.along_b[k])

    def plane2(unit, k):
        ref, rows = pick(unit, plane_rest, plane)
        row = ref.at[near.a, :, rows]
        return remote(row, row, plane2_s.at[unit, k], plane2_r.at[unit, k], near.along_a[k])

    def pack_rest():
        each(1, 8, lambda i: line_rest_copy(i).wait_recv())
        for tile in range(2):
            for i in range(8):
                packed[tile, 10 * i : 10 * i + 10, :] = line_rest[i, tile].astype(F32)[:10]
            plane_rest[near.a, near.b, tile * ROWS : (tile + 1) * ROWS] = packed[tile, :ROWS].astype(BF16)
        each(1, 4, lambda k: plane1(0, k).start())

    def across(unit):
        each(1, 4, lambda k: plane1(unit, k).wait_recv())
        each(1, 4, lambda k: plane2(unit, k).start())

    first_tile = {OPP: 2 * blocks[OPP], RIGHT: 2 * blocks[RIGHT], LEFT: 2 * blocks[LEFT], OWN: 2 * y, REST: 8}

    def held(role, tile):
        return vision_out.at[core, first_tile[role] + tile]

    def spread(unit):
        each(1, 4, lambda k: plane2(unit, k).wait_recv())
        buffer, first, n = UNITS[unit]
        rows = pl.ds(first, n)

        def move(i):
            a, b = i // 4, i % 4
            g = near.group(a, b)
            if buffer:
                vision_out[core, 2 * y + buffer - 1, g, rows] = plane[buffer - 1, a, b, rows]
            else:
                vision_out[core, 8, g] = plane_rest[a, b, :ROWS]
                vision_out[core, 9, g] = plane_rest[a, b, ROWS:]

        each(0, GROUPS, move)

    def back(piece):
        tile, first, n = PIECES[piece]
        rows = pl.ds(first, n)

        def go(role, half, i, to):
            part = held(role, tile).at[half, rows]
            return remote(part, part, back_s.at[piece, i], back_r.at[piece, i], to)

        nearer = [
            go(OWN, half_a, 0, near.right),
            go(OWN, half_b, 1, near.left),
            go(OWN, half_b, 2, near.right),
            go(OWN, half_a, 3, near.left),
        ]
        return nearer + [go(LEFT, half_a, 4, near.right), go(RIGHT, half_b, 5, near.left)]

    last = len(PIECES) - 1
    ways = [back(piece) for piece in range(len(PIECES))]

    def send_back(piece):
        spread(1 + piece)
        for copy in ways[piece][:4]:
            copy.start()
        give(OWN, piece)

    def forward(piece):
        ways[piece][0].wait_recv()
        ways[piece][4].start()
        ways[piece][1].wait_recv()
        ways[piece][5].start()

    def give_sides(piece):
        ways[piece][2].wait_recv()
        give(LEFT, piece)
        ways[piece][3].wait_recv()
        give(RIGHT, piece)

    def give_last(piece):
        ways[piece][4].wait_recv()
        ways[piece][5].wait_recv()
        give(OPP, piece)

    def mate(role, piece):
        if role == REST:
            part = held(role, piece)
        else:
            tile, first, n = PIECES[piece]
            part = held(role, tile).at[:, pl.ds(first, n)]
        return remote(part, part, mate_s.at[role, piece], mate_r.at[role, piece], near.mate)

    def give(role, piece):
        mate(role, piece).start()

    own_cols = columns(near.dp, COLS)

    def own_text():
        return pltpu.make_async_copy(text_w, text_out.at[:, own_cols], own_sem)

    def beside_copy():
        return remote(
            text_w.at[upper_rows], text_out.at[upper_rows, own_cols], spread_s.at[0, 0], spread_r.at[0, 0], near.beside
        )

    def x_copy(k):
        return remote(
            text_w.at[lower_rows], text_out.at[lower_rows, own_cols], spread_s.at[0, k], spread_r.at[0, k],
            near.along_x[k],
        )

    def upper_ways():
        def go(block, i, to):
            part = text_out.at[upper_rows, columns(block, COLS)]
            return remote(part, part, spread_s.at[1, i], spread_r.at[1, i], to)

        return [
            go(2 * x, 0, ahead),
            go(2 * x + 1, 1, behind),
            go(2 * x + 1, 2, ahead),
            go(2 * x, 3, behind),
            go(2 * near.xs[3], 4, ahead),
            go(2 * near.xs[1] + 1, 5, behind),
        ]

    upper_on = upper_ways()

    def text_spread_last():
        for i in range(2):
            upper_on[i].wait_recv()
            upper_on[4 + i].start()

    def lower_on(px):
        one = text_out.at[lower_rows, columns(2 * px + near.twin, COLS)]
        return remote(one, one, spread_s.at[2, px], spread_r.at[2, px], near.beside)

    def text_spread():
        own_text().start()
        beside_copy().start()
        x_copy(1).start()
        x_copy(3).start()

    def text_spread_on():
        own_text().wait()
        beside_copy().wait_recv()
        for copy in upper_on[:4]:
            copy.start()
        each(1, 4, lambda k: x_copy(k).wait_recv())
        each(0, 4, lambda px: lower_on(px).start())

    def start_pair(role, tile=None):
        if not tile:
            loads(role)[0].wait()
        pair(role, tile).start()

    start_pair(OPP, 0)
    start_pair(RIGHT, 0)
    add_pair(OPP, 0)
    line[0][0].start()
    line[0][1].start()
    start_pair(LEFT, 0)
    for copy in upper[:4]:
        copy.start()
    each(0, 4, lambda px: lower_copy(px).start())
    add_pair(RIGHT, 0)
    line[0][2].start()
    line[1][0].start()
    start_pair(REST)
    add_pair(LEFT, 0)
    line[0][3].start()
    line[1][1].start()
    start_pair(OWN)
    for role in (OPP, RIGHT, LEFT):
        start_pair(role, 1)
    add_rest()
    first_step(0)
    pass_on(0)
    line[1][2].start()
    line[1][3].start()
    add_own()
    arrange_states()
    text_pass_on()
    pass_on(1)
    send_states()
    for role in (OPP, RIGHT, LEFT):
        add_pair(role, 1)
    for copy in line[2][:4] + line[3][:4]:
        copy.start()
    add_line(0)
    first_step(1)
    text_middle()
    add_line(1)
    first_step(2)
    second_step(1)
    text_cross()
    pass_on(2)
    second_step(0)
    second_step(2)
    lower_x_copy(2).start()
    join_states()
    main_last(0)
    pass_on(3)
    rest_last()
    main_last(1)
    across(1)
    send_sums(0)
    add_line(2)
    first_step(3)
    across(2)
    owner_rest()
    send_back(0)
    add_line(3)
    first_step(4)
    second_step(3)
    text_last()
    text_spread()
    send_back(1)
    forward(0)
    second_step(4)
    x_copy(2).start()
    main_last(2)
    pack_rest()
    main_last(3)
    across(3)
    forward(1)
    across(4)
    across(0)
    send_back(2)
    text_spread_on()
    send_back(3)
    send_sums(1)
    give_sides(0)
    give_last(0)
    give_sides(1)
    give_last(1)
    forward(2)
    forward(3)
    text_spread_last()
    spread(0)
    give(REST, 0)
    give(REST, 1)
    give_sides(2)
    give_last(2)
    owner_main(0)
    owner_main(1)
    for r in range(10):
        for layer in range(2):
            vision_sum[r, layer : layer + 1, :] = dense[layer, r : r + 1, :]

    for role in (OPP, RIGHT, LEFT):
        for tile in range(2):
            pair(role, tile).wait_send()
    for role in (REST, OWN):
        pair(role).wait_send()
    for copies in line:
        for copy in copies:
            copy.wait_send()
    for copy in upper:
        copy.wait_send()
    each(0, 4, lambda px: lower_copy(px).wait_send())
    cross_copy().wait_send()
    each(1, 4, lambda k: lower_x_copy(k).wait_send())
    for unit in range(len(UNITS)):
        for copies in (first_copy, second_copy, plane1, plane2):
            each(1, 4, lambda k: copies(unit, k).wait_send())
    each(1, 8, lambda i: state_copy(i).wait_send())
    each(1, 8, lambda i: rest_win_copy(i).wait_send())
    for tile in range(2):
        each(1, 8, lambda i: win_copy(tile, i).wait_send())
    each(1, 8, lambda i: line_rest_copy(i).wait_send())
    beside_copy().wait_send()
    each(1, 4, lambda k: x_copy(k).wait_send())

    give_sides(3)
    give_last(3)
    for copy in upper_on[2:]:
        copy.wait_recv()
    for copy in upper_on:
        copy.wait_send()
    each(0, 4, lambda px: lower_on(px).wait())
    for copies in ways:
        for copy in copies:
            copy.wait_send()
    for role in range(5):
        for piece in range(2 if role == REST else len(PIECES)):
            mate(role, piece).wait()


def kernel_of(given):
    def run(text_hbm, vision_hbm, *refs):
        given(text_hbm, vision_hbm, refs[:3], refs[3:6], *refs[6:])

    return run


def step(text, vision, text_states, vision_states):
    rows = text.shape[0]
    up = UPPER * rows // 16
    low = rows - up
    block = (GROUPS, ROWS, COLS)
    tile = (GROUPS, ROWS, TILE)
    square = (4, 4, ROWS, TILE)
    dma = pltpu.SemaphoreType.DMA
    vmem = pltpu.VMEM
    return pl.pallas_call(
        kernel_of(step_kernel),
        name="sum_step_gather",
        out_shape=(
            jax.ShapeDtypeStruct((rows, COLS), F32),
            jax.ShapeDtypeStruct((16,) + vision_states[0].shape[1:], F32),
            jax.ShapeDtypeStruct((rows, 8 * COLS), BF16),
            jax.ShapeDtypeStruct((2, 10) + tile, BF16),
        ),
        in_specs=[pl.BlockSpec(memory_space=pltpu.HBM)] * 8,
        out_specs=[pl.BlockSpec(memory_space=pltpu.VMEM)] * 4,
        scratch_shapes=[
            vmem((5,) + block, BF16),
            vmem((5,) + block, BF16),
            vmem((5,) + block, BF16),
            vmem((2, 8, ROWS, TILE), BF16),
            vmem((2, 8, ROWS, TILE), BF16),
            vmem((2,) + tile, BF16),
            vmem((2,) + tile, BF16),
            vmem((2,) + square, BF16),
            vmem((4, 4, 2 * ROWS, TILE), BF16),
            vmem((2,) + square, BF16),
            vmem((2, 4, ROWS, TILE), BF16),
            vmem((2, 4, ROWS, TILE), BF16),
            vmem((4, 4, 2 * ROWS, TILE), BF16),
            vmem((4, 2 * ROWS, TILE), BF16),
            vmem((4, 2 * ROWS, TILE), BF16),
            vmem((4, 4, 2 * ROWS, TILE), BF16),
            vmem((4, 2) + tile, BF16),
            vmem((2, ROWS, TILE), F32),
            vmem((2, ROWS, TILE), F32),
            vmem((2, 8, 24, TILE), F32),
            vmem((2, 4, 2, 24, TILE), F32),
            vmem((2, up, COLS), BF16),
            vmem((2, up, COLS), BF16),
            vmem((2, up, COLS), BF16),
            vmem((2, 2, up, COLS), BF16),
            vmem((4, low, COLS), BF16),
            vmem((4, low, COLS), BF16),
            vmem((4, low, COLS), BF16),
            vmem((up, COLS), BF16),
            vmem((up, COLS), BF16),
            vmem((4, low, COLS), BF16),
            vmem((3, rows, COLS), F32),
            vmem((4,) + vision_states[0].shape, F32),
            vmem((2, 40, 5 * COLS), F32),
            vmem((8, 40, COLS), F32),
            vmem((3, ROWS + 8, COLS), F32),
            vmem((2, 24, 5 * COLS), F32),
            vmem((2, 2, 16, TILE), BF16),
            vmem((8, 2, 16, TILE), BF16),
            vmem((2, ROWS + 8, TILE), F32),
            vmem((rows, COLS), BF16),
            vmem((2,) + square, BF16),
            dma((5, 2)),
            dma((8,)),
            dma((3, 2)),
            dma((5, 2)), dma((5, 2)),
            dma((4, 6)), dma((4, 6)),
            dma((6, 4)), dma((6, 4)),
            dma((6, 4)), dma((6, 4)),
            dma((8,)), dma((8,)),
            dma((2, 8)), dma((2, 8)),
            dma((8,)), dma((8,)),
            dma((6,)), dma((6,)),
            dma((4,)), dma((4,)),
            dma((4,)), dma((4,)),
            dma((8,)), dma((8,)),
            dma((6, 4)), dma((6, 4)),
            dma((6, 4)), dma((6, 4)),
            dma((4, 6)), dma((4, 6)),
            dma((5, 4)), dma((5, 4)),
            dma((3, 6)), dma((3, 6)),
            dma,
        ],
        compiler_params=pltpu.CompilerParams(collective_id=1, has_side_effects=True, vmem_limit_bytes=40 << 20),
    )(*[pltpu.with_memory_space_constraint(array, pltpu.HBM) for array in (text, vision, *text_states, *vision_states)])


def finish_kernel(*refs):
    text, vision, text_full, vision_full = refs[:5], refs[5:10], refs[10], refs[11]
    outs, vision_w = refs[12:22], refs[21]
    text_made, vision_made, vision_in, sem, tile_sem, in_sem = refs[22:]
    text_w = outs[4]
    copies = [
        pltpu.make_async_copy(vision_full.at[layer, t], vision_w.at[layer, :, :, t * TILE : (t + 1) * TILE], tile_sem.at[layer, t])
        for layer in range(2)
        for t in range(10)
    ]
    copies.append(pltpu.make_async_copy(text_full, text_w, sem.at[1]))
    rows_in = vision_made.shape[1]
    taken = [pltpu.make_async_copy(ref.at[:rows_in], vision_in.at[k], in_sem.at[k]) for k, ref in enumerate(vision)]
    for copy in taken + copies:
        copy.start()

    def one(i):
        rows = pl.ds(pl.multiple_of(i * 32, 32), 32)
        made = adam_step(*[ref[rows] for ref in text])
        for j in range(4):
            text_made[j, rows] = made[j]

    loop(0, text_made.shape[1] // 32, one)
    for j in range(4):
        copies.append(pltpu.make_async_copy(text_made.at[j], outs[j], sem.at[2 + j]))
        copies[-1].start()

    for copy in taken:
        copy.wait()

    def row(r):
        made = adam_step(*[vision_in[k, r] for k in range(5)])
        for j in range(4):
            vision_made[j, r] = made[j]

    loop(0, vision_made.shape[1], row)
    for j in range(4):
        copies.append(pltpu.make_async_copy(vision_made.at[j], outs[5 + j], sem.at[6 + j]))
        copies[-1].start()
    for copy in copies:
        copy.wait()


def finish(text, vision, text_full, vision_full):
    def like(array):
        return jax.ShapeDtypeStruct(array.shape, array.dtype)

    in_hbm, in_vmem = pl.BlockSpec(memory_space=pltpu.HBM), pl.BlockSpec(memory_space=pltpu.VMEM)
    return pl.pallas_call(
        finish_kernel,
        name="write_results",
        out_shape=(like(text[0]),) * 4
        + (like(text_full),)
        + (like(vision[1]),) * 4
        + (jax.ShapeDtypeStruct((2, GROUPS, ROWS, 5 * COLS), BF16),),
        in_specs=[in_vmem] * 5 + [in_hbm] * 7,
        out_specs=[in_hbm] * 10,
        scratch_shapes=[
            pltpu.VMEM((4,) + text[0].shape, F32),
            pltpu.VMEM((5,) + vision[1].shape, F32),
            pltpu.VMEM((6,) + vision[1].shape, F32),
            pltpu.SemaphoreType.DMA((10,)),
            pltpu.SemaphoreType.DMA((2, 10)),
            pltpu.SemaphoreType.DMA((5,)),
        ],
        compiler_params=pltpu.CompilerParams(vmem_limit_bytes=16 << 20),
    )(*text, *vision, text_full, vision_full)


def body(
    text_grads, text_master, text_moment, text_second, text_ref,
    vision_grads, vision_master, vision_moment, vision_second, vision_ref,
):
    layers, width = vision_grads.shape[1], vision_grads.shape[3]
    text_states = (text_moment, text_second, text_master, text_ref)
    vision_states = tuple(
        jnp.transpose(array, (1, 0, 2)) for array in (vision_moment, vision_second, vision_master, vision_ref)
    )
    text_total, vision_total, text_full, vision_full = step(
        text_grads[0], vision_grads.reshape(layers, GROUPS, ROWS, width), text_states[:3], vision_states[:3]
    )
    outs = finish((text_total,) + text_states, (vision_total,) + vision_states, text_full, vision_full)
    vision_out = tuple(jnp.transpose(array, (1, 0, 2)) for array in outs[5:9])
    return outs[:5] + vision_out + (outs[9].reshape(layers, width, width),)


def solution(mesh):
    owned = P("tensor", "dp")
    vision_owned = P(None, ("dp", "tensor"), None)
    return jax.shard_map(
        body,
        mesh=mesh,
        in_specs=(P("dp", "tensor", None),) + (owned,) * 4 + (P(("dp", "tensor"), None, None, None),) + (vision_owned,) * 4,
        out_specs=(owned,) * 4 + (P("tensor", None),) + (vision_owned,) * 4 + (P(),),
        check_vma=False,
    )
```
